256 devices in a mesh: gy: 16 (over z_hi, x), gz: 16 (over y, z_lo, core).
Axes of the slice: x: 4, y: 4, z: 8 (z_hi: 4, z_lo: 2; z = z_hi * 2 + z_lo), core: 2. Of those that a mesh axis runs over, the one named last changes fastest.
Arguments:
- field: bfloat16 [4, 512, 512, 512], P(None, 'gy', 'gz'), may hold values from -300 to 300
- basis_one: bfloat16 [512, 96], replicated, may hold values from -0.25 to 0.25
- basis_two: bfloat16 [512, 96], P('gy'), may hold values from -0.25 to 0.25
- basis_three: bfloat16 [512, 96], P('gz'), may hold values from -0.25 to 0.25
Outputs:
- gram_one: float32 [512, 512], P(('gy', 'gz'))
- gram_two: float32 [512, 512], P(('gy', 'gz'))
- core: float32 [4, 96, 96, 96], P(None, 'gy', 'gz')
The draws below stay inside these ranges and needn't reach their ends.
All inputs are finite; a program needn't handle non-finite values.
Results may differ from the reference program's by a relative error of at most 0.0045.
Values may be sent and summed in bfloat16 or wider, within the bound.
No kernel may reach another device: no remote copies, remote signals or barrier semaphores. Data moves between devices by JAX's collectives and lax.ppermute only.
A program may use at most 64 MiB of HBM per device.

```python
import jax
import jax.numpy as jnp
from jax import lax

V = 4
N1 = 512
R = 96
N2 = 512
N3 = 512


def draw_field(key, part):
    key = jax.random.fold_in(key, 11)
    keys = jax.random.split(key, 9)
    mode_count = 48
    base_noise = jnp.clip(jax.random.normal(keys[0], (V, N2, N3, N1), jnp.float32), -6.0, 6.0)
    var_loads = jnp.clip(jax.random.normal(keys[5], (V, mode_count), jnp.float32), -3.0, 3.0)
    second_loads = jnp.clip(jax.random.normal(keys[6], (N2, mode_count), jnp.float32), -3.0, 3.0)
    third_loads = jnp.clip(jax.random.normal(keys[7], (N3, mode_count), jnp.float32), -3.0, 3.0)
    first_loads = jnp.clip(jax.random.normal(keys[8], (mode_count, N1), jnp.float32), -3.0, 3.0) / jnp.sqrt(jnp.float32(mode_count))
    spatial = var_loads[:, None, None, :] * second_loads[None, :, None, :] * third_loads[None, None, :, :]
    structured = jnp.dot(spatial.reshape(-1, mode_count), first_loads, precision=lax.Precision.HIGHEST)
    structured = jnp.clip(structured.reshape(V, N2, N3, N1), -8.0, 8.0)
    row_scale = 10.0 ** jax.random.uniform(keys[1], (N1,), jnp.float32) / 3.1623
    ramp_two = (1.0 + 2.0 * jnp.arange(N2, dtype=jnp.float32) / N2) * 0.5
    ramp_two = ramp_two * jnp.exp(jax.random.uniform(keys[2], (N2,), jnp.float32, -0.35, 0.35))
    ramp_three = (1.0 + 2.0 * jnp.arange(N3, dtype=jnp.float32) / N3) * 0.5
    ramp_three = ramp_three * jnp.exp(jax.random.uniform(keys[3], (N3,), jnp.float32, -0.35, 0.35))
    var_scale = jnp.exp(jax.random.uniform(keys[4], (V,), jnp.float32, -0.3, 0.3))
    combined = base_noise + structured
    values = combined * var_scale[:, None, None, None] * ramp_two[None, :, None, None] * ramp_three[None, None, :, None] * row_scale[None, None, None, :]
    return values.astype(jnp.bfloat16)


def steps_of(rng, dims, pieces, low, largest):
    level = 1.0
    for position, parts in pieces:
        steps = jax.random.uniform(jax.random.fold_in(jax.random.fold_in(rng, 6), position), (parts,), jnp.float32, low / len(pieces), largest / len(pieces))
        level = level * jnp.repeat(jnp.exp(steps), dims[position] // parts).reshape((-1,) + (1,) * (len(dims) - 1 - position))
    return level


def noise(key, dims, deviation, reach, cuts=(), held_as=jnp.bfloat16):
    result = jax.random.normal(key, dims, jnp.float32) * deviation
    if len(cuts) > 0:
        result = steps_of(key, dims, cuts, -0.22, 0.18) * result
    return jnp.clip(result, min=-reach, max=reach).astype(held_as)


def setup_inputs(seed: int = 0) -> dict:
    seeds = jax.random.split(jax.random.key(seed), 5)
    return {
        "field": draw_field(jax.random.fold_in(seeds[4], 71), 0),
        "basis_one": noise(seeds[1], (N1, R), N1 ** -0.5, 0.25),
        "basis_two": noise(seeds[2], (N2, R), N2 ** -0.5, 0.25, ((0, 16),)),
        "basis_three": noise(seeds[3], (N3, R), N3 ** -0.5, 0.25, ((0, 16),)),
    }


def reference(field, basis_one, basis_two, basis_three):
    flattened = field.reshape(-1, N1)
    gram_one = jnp.dot(flattened.T, flattened, preferred_element_type=jnp.float32) / (V * N2 * N3)
    truncated = jnp.dot(flattened, basis_one, preferred_element_type=jnp.float32).astype(jnp.bfloat16)
    truncated = truncated.reshape(V, N2, N3, R)
    widened = truncated.astype(jnp.float32)
    gram_two = jnp.einsum("vjkr,vmkr->jm", widened, widened, precision=lax.Precision.HIGHEST) / (V * N3 * R)
    mixed_two = jnp.einsum("vjkr,js->vskr", widened, basis_two.astype(jnp.float32), precision=lax.Precision.HIGHEST)
    core = jnp.einsum("vskr,kt->vstr", mixed_two, basis_three.astype(jnp.float32), precision=lax.Precision.HIGHEST)
    return gram_one, gram_two, core
```

```python
import jax
import jax.numpy as jnp
from jax import lax
from jax.experimental import pallas as pl
from jax.experimental.pallas import tpu as pltpu
from jax.sharding import PartitionSpec as P

F32 = jnp.float32
BF16 = jnp.bfloat16
LIMIT = 48 * 1024 * 1024


def nt_dot(a, b):
    return lax.dot_general(a, b, (((1,), (1,)), ((), ())), preferred_element_type=F32)


def truncate_kernel(b1t_ref, field_ref, out_ref, rows, tiles):
    cells = field_ref[0].reshape(1024, 512)
    trunc = nt_dot(b1t_ref[...], cells)
    for b in range(8):
        rows[pl.ds(b, 96, stride=8), :] = trunc[:, b * 128 : (b + 1) * 128]
    lane = lax.broadcasted_iota(jnp.int32, (8, 128), 1) // 32
    for block in range(24):
        part = [rows[(block * 4 + rr) * 8 : (block * 4 + rr) * 8 + 8, :] for rr in range(4)]
        for jj in range(4):
            moved = [
                part[rr] if rr == jj else pltpu.roll(part[rr], (32 * (rr - jj)) % 128, 1)
                for rr in range(4)
            ]
            low = jnp.where(lane == 0, moved[0], moved[1])
            high = jnp.where(lane == 2, moved[2], moved[3])
            tiles[pl.ds(block * 32 + jj, 8, stride=4), :] = jnp.where(lane < 2, low, high)
    out_ref[...] = tiles[...].astype(BF16).reshape(4, 6, 32, 128)


def truncate(b1t, field):
    return pl.pallas_call(
        truncate_kernel,
        out_shape=jax.ShapeDtypeStruct((16, 6, 32, 128), BF16),
        grid=(4,),
        in_specs=[
            pl.BlockSpec((96, 512), lambda v: (0, 0)),
            pl.BlockSpec((1, 32, 32, 512), lambda v: (v, 0, 0, 0)),
        ],
        out_specs=pl.BlockSpec((4, 6, 32, 128), lambda v: (v, 0, 0, 0)),
        scratch_shapes=[pltpu.VMEM((768, 128), F32), pltpu.VMEM((768, 128), F32)],
        compiler_params=pltpu.CompilerParams(vmem_limit_bytes=LIMIT),
    )(b1t, field)


def partial_kernel(whole_ref, b2t_ref, kron_ref, one_ref, out_ref, gram):
    x = jnp.concatenate([whole_ref[:, a].reshape(512, 128) for a in range(6)], axis=1)
    mixed = jnp.dot(b2t_ref[...], x, preferred_element_type=F32).astype(BF16)
    for gz in range(16):
        part = nt_dot(kron_ref[gz * 144 : (gz + 1) * 144, :], mixed)
        out_ref[gz, 256:400, :] = part.astype(BF16)

    def scatter(values, first):
        for c in range(4):
            gram[c * 512 : (c + 1) * 512, :] = values[:, c * 128 : (c + 1) * 128]
        for gz in range(16):
            for c in range(4):
                for e in range(2):
                    at = first + c * 32 + e * 16
                    rows = gram[pl.ds(c * 512 + gz * 2 + e, 16, stride=32), :]
                    out_ref[gz, at : at + 16, :] = rows.astype(BF16)

    scatter(nt_dot(x, x), 128)
    scatter(one_ref[...], 0)


def partials(whole, b2t, kron, one):
    return pl.pallas_call(
        partial_kernel,
        out_shape=jax.ShapeDtypeStruct((16, 400, 128), BF16),
        scratch_shapes=[pltpu.VMEM((2048, 128), F32)],
        compiler_params=pltpu.CompilerParams(vmem_limit_bytes=LIMIT),
    )(whole, b2t, kron, one)


def middle_kernel(in_ref, out_ref, core, cut):
    total = in_ref[0].astype(F32)
    for source in range(1, 16):
        total = total + in_ref[source].astype(F32)
    cut[...] = jnp.zeros_like(cut)
    for first in range(2):
        for c in range(4):
            for e in range(2):
                at = first * 128 + c * 32 + e * 16
                cut[pl.ds(first * 8 + e * 4 + c, 16, stride=32), :] = total[at : at + 16]
    core[0:128, :] = total[256:384].T
    tail = jnp.concatenate([total[384:400], jnp.zeros((112, 128), F32)], axis=0)
    core[128:256, :] = tail.T
    for s in range(6):
        cut[pl.ds(16 + s, 16, stride=32), :] = core[pl.ds(s, 16, stride=6), :]
        cut[pl.ds(22 + s, 16, stride=32), :] = core[pl.ds(128 + s, 16, stride=6), :]
    out_ref[...] = cut[...].astype(BF16).reshape(16, 32, 128)


def middle(received):
    return pl.pallas_call(
        middle_kernel,
        out_shape=jax.ShapeDtypeStruct((16, 32, 128), BF16),
        scratch_shapes=[pltpu.VMEM((256, 128), F32), pltpu.VMEM((512, 128), F32)],
        compiler_params=pltpu.CompilerParams(vmem_limit_bytes=LIMIT),
    )(received)


def last_kernel(scale_one, scale_two, in_ref, one_ref, two_ref, core_ref):
    total = in_ref[0, 0:16, :].astype(F32)
    for source in range(1, 16):
        total = total + in_ref[source, 0:16, :].astype(F32)
    for e in range(2):
        for c in range(4):
            lanes = slice(c * 128, (c + 1) * 128)
            one_ref[e : e + 1, lanes] = total[e * 4 + c : e * 4 + c + 1] * scale_one
            two_ref[e : e + 1, lanes] = total[8 + e * 4 + c : 9 + e * 4 + c] * scale_two
    lane = lax.broadcasted_iota(jnp.int32, (16, 128), 1)
    for v in range(4):
        blocks = [in_ref[v * 4 + g, 16:32, :].astype(F32) for g in range(4)]
        for t in range(6):
            row = jnp.zeros((16, 128), F32)
            for g in range(4):
                shift = (24 * (g - t)) % 128
                moved = pltpu.roll(blocks[g], shift, 1) if shift else blocks[g]
                if t == 5:
                    rest = jnp.concatenate([blocks[g][6:16], blocks[g][0:6]], axis=0)
                    rest = pltpu.roll(rest, 24 * g + 8, 1)
                    moved = jnp.where(lane < 24 * g + 8, moved, rest)
                row = jnp.where((lane >= 24 * g) & (lane < 24 * g + 24), moved, row)
            for s in range(6):
                core_ref[s, t, v : v + 1, :] = row[s : s + 1, 0:96]


def last(received, scale_one, scale_two):
    def body(*refs):
        last_kernel(scale_one, scale_two, *refs)

    return pl.pallas_call(
        body,
        out_shape=(
            jax.ShapeDtypeStruct((2, 512), F32),
            jax.ShapeDtypeStruct((2, 512), F32),
            jax.ShapeDtypeStruct((6, 6, 4, 96), F32),
        ),
        compiler_params=pltpu.CompilerParams(vmem_limit_bytes=LIMIT),
    )(received)


def gather_two(basis_two):
    me = lax.axis_index("gy")

    def ring(block, place, neighbour):
        got = [block]
        for step in range(1, 4):
            got.append(lax.ppermute(block, "gy", [(i, neighbour(i, step)) for i in range(16)]))
        turned = jnp.concatenate(got[::-1] + got[::-1], axis=0)
        size = block.shape[0]
        return lax.dynamic_slice_in_dim(turned, (3 - place) * size, 4 * size, axis=0)

    near = ring(basis_two, me % 4, lambda i, d: i // 4 * 4 + (i + d) % 4)
    return ring(near, me // 4, lambda i, d: (i + 4 * d) % 16)


def shards(field, basis_one, basis_two, basis_three):
    sent = truncate(basis_one.T, field)
    whole = lax.all_to_all(sent, "gy", split_axis=0, concat_axis=0, tiled=True)
    flattened = field.reshape(-1, 512)
    one = jnp.dot(flattened.T, flattened, preferred_element_type=F32)
    b2t = jnp.pad(gather_two(basis_two).T, ((0, 32), (0, 0)))
    repeated = jnp.tile(basis_three.T, (1, 24))[:, None, :]
    same = jnp.arange(24)[:, None] == jnp.arange(768)[None, :] // 32
    kron = jnp.where(same[None], repeated, jnp.zeros((), BF16)).reshape(2304, 768)
    blocks = partials(whole, b2t, kron, one)
    blocks = lax.all_to_all(blocks, "gz", split_axis=0, concat_axis=0, tiled=True)
    blocks = middle(blocks)
    blocks = lax.all_to_all(blocks, "gy", split_axis=0, concat_axis=0, tiled=True)
    gram_one, gram_two, core = last(blocks, 1.0 / 1048576, 1.0 / 196608)
    return (gram_one, gram_two, jnp.transpose(core, (2, 0, 1, 3)))


def solution(mesh):
    in_specs = (P(None, "gy", "gz", None), P(), P("gy", None), P("gz", None))
    out_specs = (P(("gy", "gz"), None), P(("gy", "gz"), None), P(None, "gy", "gz", None))
    return jax.shard_map(shards, mesh=mesh, in_specs=in_specs, out_specs=out_specs, check_vma=False)
```

```python
import jax
import jax.numpy as jnp
from jax import lax
from jax.experimental import pallas as pl
from jax.experimental.pallas import tpu as pltpu
from jax.sharding import PartitionSpec as P

F32 = jnp.float32
BF16 = jnp.bfloat16
WIDE = 60 * 1024 * 1024
LIMIT = 48 * 1024 * 1024
VMEM = pl.BlockSpec(memory_space=pltpu.VMEM)
HBM = pl.BlockSpec(memory_space=pltpu.HBM)
ANY = pl.BlockSpec(memory_space=pl.ANY)


def nt_dot(a, b):
    return lax.dot_general(a, b, (((1,), (1,)), ((), ())), preferred_element_type=F32)


def call(kernel, outs, scratch=(), specs=None, limit=LIMIT, out_specs=None, name=None):
    keywords = {} if out_specs is None else {"out_specs": out_specs}
    return lambda *args: pl.pallas_call(
        kernel,
        out_shape=outs,
        in_specs=[VMEM] * len(args) if specs is None else specs,
        scratch_shapes=list(scratch),
        compiler_params=pltpu.CompilerParams(vmem_limit_bytes=limit),
        name=name,
        **keywords,
    )(*args)


def shape(dims, dtype=BF16):
    return jax.ShapeDtypeStruct(dims, dtype)


def truncate_kernel(b1t_ref, b2_ref, field_ref, out_ref, b1t, b2, b2_wide, cells, rows, tiles, sent, sems):
    core = lax.axis_index("gz") % 2
    small = [
        pltpu.make_async_copy(b1t_ref, b1t, sems.at[0]),
        pltpu.make_async_copy(b2_ref, b2, sems.at[1]),
    ]
    for copy in small:
        copy.start()
    copies = []
    for piece in range(8):
        v, half = piece // 2, pl.ds(piece % 2 * 16, 16)
        copies.append(
            pltpu.make_async_copy(field_ref.at[v, half], cells.at[v, half], sems.at[2 + piece])
        )
        copies[-1].start()
    for copy in small:
        copy.wait()
    b2_wide[...] = jnp.zeros_like(b2_wide)
    b2_wide[:, 0:96] = b2[...].astype(F32)
    share = [b2_wide[pl.ds(core * 2 + e, 8, stride=4), :] for e in range(2)]
    share = jnp.concatenate(share, axis=0).astype(BF16)
    for peer in range(16):
        sent[peer, 192:208, :] = share
    lane = lax.broadcasted_iota(jnp.int32, (8, 128), 1) // 32
    outs = []
    for v in range(4):
        for half in range(2):
            copies[v * 2 + half].wait()
            trunc = nt_dot(b1t[...], cells[v, half * 16 : half * 16 + 16].reshape(512, 512))
            for b in range(4):
                rows[pl.ds(half * 4 + b, 96, stride=8), :] = trunc[:, b * 128 : (b + 1) * 128]
        for block in range(24):
            first = block * 32
            part = [rows[first + rr * 8 : first + rr * 8 + 8, :] for rr in range(4)]
            for jj in range(4):
                moved = [
                    part[rr] if rr == jj else pltpu.roll(part[rr], (32 * (rr - jj)) % 128, 1)
                    for rr in range(4)
                ]
                low = jnp.where(lane == 0, moved[0], moved[1])
                high = jnp.where(lane == 2, moved[2], moved[3])
                tiles[first + jj * 8 : first + jj * 8 + 8, :] = jnp.where(lane < 2, low, high)
        block = slice(v * 4, v * 4 + 4)
        sent[block, 0:192, :] = tiles[...].astype(BF16).reshape(4, 192, 128)
        outs.append(pltpu.make_async_copy(sent.at[block], out_ref.at[block], sems.at[10 + v]))
        outs[-1].start()
    for copy in outs:
        copy.wait()


truncate = call(
    truncate_kernel,
    shape((16, 208, 128)),
    [
        pltpu.VMEM((96, 512), BF16),
        pltpu.VMEM((32, 96), BF16),
        pltpu.VMEM((32, 128), F32),
        pltpu.VMEM((4, 32, 32, 512), BF16),
        pltpu.VMEM((768, 128), F32),
        pltpu.VMEM((768, 128), F32),
        pltpu.VMEM((16, 208, 128), BF16),
        pltpu.SemaphoreType.DMA((14,)),
    ],
    [HBM, HBM, HBM],
    WIDE,
    HBM,
    "truncate",
)


def split_kernel(one_ref, other_ref, own_ref, gram):
    core = lax.axis_index("gz") % 2
    for c in range(4):
        gram[c * 512 : (c + 1) * 512, :] = one_ref[:, c * 128 : (c + 1) * 128]
    for out_ref, side in ((other_ref, 1 - core), (own_ref, core)):
        for b in range(8):
            for c in range(4):
                for e in range(2):
                    at = c * 32 + e * 16
                    rows = gram[pl.ds(c * 512 + b * 4 + side * 2 + e, 16, stride=32), :]
                    out_ref[b // 2, b % 2, at : at + 16, :] = rows.astype(BF16)


split = call(
    split_kernel,
    (shape((4, 2, 128, 128)), shape((4, 2, 128, 128))),
    [pltpu.VMEM((2048, 128), F32)],
    name="split",
)


def along_y_kernel(own_ref, got_ref, *out_refs):
    y = lax.axis_index("gz") // 4
    for distance, out_ref in enumerate(out_refs):
        at = lax.rem(y + distance, 4)
        out_ref[...] = (own_ref[at].astype(F32) + got_ref[at].astype(F32)).astype(BF16)


along_y = call(along_y_kernel, tuple(shape((2, 128, 128)) for _ in range(4)), name="along_y")


def along_z_kernel(*refs):
    other_ref, own_ref = refs[4:]
    place = lax.axis_index("gz") // 2 % 2
    for out_ref, at in ((other_ref, 1 - place), (own_ref, place)):
        total = refs[0][at].astype(F32)
        for ref in refs[1:4]:
            total = total + ref[at].astype(F32)
        out_ref[...] = total.astype(BF16)


along_z = call(along_z_kernel, (shape((128, 128)), shape((128, 128))), name="along_z")


def gram_kernel(whole_ref, *refs):
    other_ref, own_ref, gram = refs[-3:]
    core = lax.axis_index("gz") % 2

    def cells(first, size):
        parts = [whole_ref[:, pl.ds(a * 32 + first, size), :] for a in range(6)]
        return jnp.concatenate([part.reshape(16 * size, 128) for part in parts], axis=1)

    x = cells(0, 32)
    for out_ref, side in ((other_ref, 1 - core), (own_ref, core)):
        values = nt_dot(cells(pl.multiple_of(side * 16, 16), 16), x)
        for c in range(4):
            gram[c * 256 : (c + 1) * 256, :] = values[:, c * 128 : (c + 1) * 128]
        for b in range(8):
            for c in range(4):
                rows = gram[pl.ds(c * 256 + b, 32, stride=8), :]
                out_ref[b, c * 32 : c * 32 + 32, :] = rows.astype(BF16)


gram_part = call(
    gram_kernel,
    (shape((8, 128, 128)), shape((8, 128, 128))),
    [pltpu.VMEM((1024, 128), F32)],
    [VMEM] + [ANY] * 4,
    name="gram_part",
)


def core_kernel(whole_ref, got_ref, kron_ref, after_ref, other_ref, own_ref, basis, parts):
    core = lax.axis_index("gz") % 2
    basis[:, core] = whole_ref[:, 192:208, :]
    basis[:, 1 - core] = got_ref[...]
    x = [whole_ref[:, a * 32 : (a + 1) * 32, :].reshape(512, 128) for a in range(6)]
    mixed = lax.dot_general(
        basis[...].reshape(512, 128),
        jnp.concatenate(x, axis=1),
        (((0,), (0,)), ((), ())),
        preferred_element_type=F32,
    )
    high = mixed.astype(BF16)
    low = (mixed - high.astype(F32)).astype(BF16)
    for a in range(3):
        lanes = slice(a * 256, (a + 1) * 256)
        parts[a] = nt_dot(kron_ref[...], high[:, lanes]) + nt_dot(kron_ref[...], low[:, lanes])
    for out_ref, side in ((other_ref, 1 - core), (own_ref, core)):
        for b in range(8):
            pieces = []
            for t in range(6):
                at = pl.multiple_of((side + b * 2) * 48 + t * 8, 8)
                pieces += [parts[a, pl.ds(at, 8), :] for a in range(3)]
            out_ref[b] = jnp.concatenate(pieces, axis=0).astype(out_ref.dtype)


core_part = call(
    core_kernel,
    (shape((8, 144, 128)), shape((8, 144, 128), F32)),
    [pltpu.VMEM((16, 2, 16, 128), BF16), pltpu.VMEM((3, 768, 128), F32)],
    [VMEM, VMEM, VMEM, ANY],
    name="core_part",
)


def pair_kernel(gram_ref, gram_got_ref, core_ref, core_got_ref, out_ref):
    out_ref[:, 0:128, :] = (gram_ref[...].astype(F32) + gram_got_ref[...].astype(F32)).astype(BF16)
    out_ref[:, 128:272, :] = (core_ref[...] + core_got_ref[...].astype(F32)).astype(BF16)


pair = call(pair_kernel, shape((8, 272, 128)), name="pair")


def middle_kernel(in_ref, one_ref, one_got_ref, out_ref, sums, core, cut):
    total = in_ref[0].astype(F32)
    for source in range(1, 8):
        total = total + in_ref[source].astype(F32)
    sums[...] = total[0:128]
    cut[...] = jnp.zeros_like(cut)
    one = one_ref[...].astype(F32) + one_got_ref[...].astype(F32)
    for c in range(4):
        for e in range(2):
            at = c * 32 + e * 16
            cut[pl.ds(e * 4 + c, 16, stride=32), :] = one[at : at + 16]
            cut[pl.ds(8 + e * 4 + c, 16, stride=32), :] = sums[pl.ds(c * 32 + e, 16, stride=2), :]
    core[0:128, :] = total[128:256].T
    tail = jnp.concatenate([total[256:272], jnp.zeros((112, 128), F32)], axis=0)
    core[128:256, :] = tail.T
    for s in range(6):
        cut[pl.ds(16 + s, 16, stride=32), :] = core[pl.ds(s, 16, stride=6), :]
        cut[pl.ds(22 + s, 16, stride=32), :] = core[pl.ds(128 + s, 16, stride=6), :]
    out_ref[...] = cut[...].astype(BF16).reshape(16, 32, 128)


middle = call(
    middle_kernel,
    shape((16, 32, 128)),
    [pltpu.VMEM((128, 128), F32), pltpu.VMEM((256, 128), F32), pltpu.VMEM((512, 128), F32)],
    name="middle",
)


def last_kernel(scale_one, scale_two, in_ref, one_ref, two_ref, core_ref, turned, ordered):
    total = in_ref[0, 0:16, :].astype(F32)
    for source in range(1, 16):
        total = total + in_ref[source, 0:16, :].astype(F32)
    turned[...] = jnp.concatenate([total[8:16], jnp.zeros((120, 128), F32)], axis=0).T
    for group in range(4):
        for jj in range(4):
            rows = turned[group * 32 + jj * 8 : group * 32 + jj * 8 + 8, :]
            ordered[pl.ds(group * 32 + jj, 8, stride=4), :] = rows
    two = ordered[...].T
    for e in range(2):
        for c in range(4):
            lanes = slice(c * 128, (c + 1) * 128)
            one_ref[e : e + 1, lanes] = total[e * 4 + c : e * 4 + c + 1] * scale_one
            two_ref[e : e + 1, lanes] = two[e * 4 + c : e * 4 + c + 1] * scale_two
    lane = lax.broadcasted_iota(jnp.int32, (16, 128), 1)
    for v in range(4):
        blocks = [in_ref[v * 4 + g, 16:32, :].astype(F32) for g in range(4)]
        for t in range(6):
            row = jnp.zeros((16, 128), F32)
            for g in range(4):
                shift = (24 * (g - t)) % 128
                moved = pltpu.roll(blocks[g], shift, 1) if shift else blocks[g]
                if t == 5:
                    rest = jnp.concatenate([blocks[g][6:16], blocks[g][0:6]], axis=0)
                    rest = pltpu.roll(rest, 24 * g + 8, 1)
                    moved = jnp.where(lane < 24 * g + 8, moved, rest)
                row = jnp.where((lane >= 24 * g) & (lane < 24 * g + 24), moved, row)
            for s in range(6):
                core_ref[s, t, v : v + 1, :] = row[s : s + 1, 0:96]


def last(received, scale_one, scale_two):
    def body(*refs):
        last_kernel(scale_one, scale_two, *refs)

    outs = (shape((2, 512), F32), shape((2, 512), F32), shape((6, 6, 4, 96), F32))
    scratch = [pltpu.VMEM((128, 128), F32)] * 2
    return call(body, outs, scratch, name="last")(received)


def along_gz(y, z_lo, core):
    return [
        (i, (i // 4 + y) % 4 * 4 + (i // 2 % 2 ^ z_lo) * 2 + (i % 2 ^ core)) for i in range(16)
    ]


def send(block, y=0, z_lo=0, core=0):
    return lax.ppermute(block, "gz", along_gz(y, z_lo, core))


def shards(field, basis_one, basis_two, basis_three):
    sent = truncate(basis_one.T, basis_two, field)
    sent, field, basis_three = lax.optimization_barrier((sent, field, basis_three))
    whole = lax.all_to_all(sent, "gy", split_axis=0, concat_axis=0, tiled=True)

    flattened = field.reshape(-1, 512)
    one = jnp.dot(flattened.T, flattened, preferred_element_type=F32)
    other, own = split(one)
    blocks = along_y(own, send(other, core=1))
    blocks = [blocks[0]] + [send(blocks[d], y=d) for d in range(1, 4)]
    other, one_own = along_z(*blocks)
    one_got = send(other, z_lo=1)

    repeated = jnp.tile(basis_three.T, (1, 8))[:, None, :]
    same = jnp.arange(8)[:, None] == jnp.arange(256)[None, :] // 32
    kron = jnp.where(same[None], repeated, jnp.zeros((), BF16)).reshape(768, 256)

    basis_got = send(whole[:, 192:208], core=1)
    gram_other, gram_own = gram_part(whole, *blocks)
    gram_got = send(gram_other, core=1)
    core_other, core_own = core_part(whole, basis_got, kron, gram_other)
    core_got = send(core_other, core=1)
    summed = pair(gram_own, gram_got, core_own, core_got)
    groups = [[2 * b + core for b in range(8)] for core in range(2)]
    summed = lax.all_to_all(
        summed, "gz", split_axis=0, concat_axis=0, tiled=True, axis_index_groups=groups
    )
    cut = middle(summed, one_own, one_got)
    cut = lax.all_to_all(cut, "gy", split_axis=0, concat_axis=0, tiled=True)
    gram_one, gram_two, core = last(cut, 1.0 / 1048576, 1.0 / 196608)
    return (gram_one, gram_two, jnp.transpose(core, (2, 0, 1, 3)))


def solution(mesh):
    in_specs = (P(None, "gy", "gz", None), P(), P("gy", None), P("gz", None))
    out_specs = (P(("gy", "gz"), None), P(("gy", "gz"), None), P(None, "gy", "gz", None))
    return jax.shard_map(shards, mesh=mesh, in_specs=in_specs, out_specs=out_specs, check_vma=False)
```

```python
import functools

import jax
import jax.numpy as jnp
from jax import lax
from jax.experimental import pallas as pl
from jax.experimental.pallas import tpu as pltpu
from jax.sharding import PartitionSpec as P

F32 = jnp.float32
BF16 = jnp.bfloat16
WIDE = 60 * 1024 * 1024
LIMIT = 48 * 1024 * 1024
VMEM = pl.BlockSpec(memory_space=pltpu.VMEM)
HBM = pl.BlockSpec(memory_space=pltpu.HBM)
ANY = pl.BlockSpec(memory_space=pl.ANY)


def nt_dot(a, b):
    return lax.dot_general(a, b, (((1,), (1,)), ((), ())), preferred_element_type=F32)


def call(kernel, outs, scratch=(), specs=None, limit=LIMIT, out_specs=None, name=None):
    keywords = {} if out_specs is None else {"out_specs": out_specs}
    return lambda *args: pl.pallas_call(
        kernel,
        out_shape=outs,
        in_specs=[VMEM] * len(args) if specs is None else specs,
        scratch_shapes=list(scratch),
        compiler_params=pltpu.CompilerParams(vmem_limit_bytes=limit),
        name=name,
        **keywords,
    )(*args)


def shape(dims, dtype=BF16):
    return jax.ShapeDtypeStruct(dims, dtype)


def truncate_kernel(b1t_ref, b2_ref, field_ref, out_ref, b1t, b2, b2_wide, cells, rows, tiles, sent, sems):
    core = lax.axis_index("gz") % 2
    small = [
        pltpu.make_async_copy(b1t_ref, b1t, sems.at[0]),
        pltpu.make_async_copy(b2_ref, b2, sems.at[1]),
    ]
    for copy in small:
        copy.start()
    copies = []
    for piece in range(8):
        v, half = piece // 2, pl.ds(piece % 2 * 16, 16)
        copies.append(
            pltpu.make_async_copy(field_ref.at[v, half], cells.at[v, half], sems.at[2 + piece])
        )
        copies[-1].start()
    for copy in small:
        copy.wait()
    b2_wide[...] = jnp.zeros_like(b2_wide)
    b2_wide[:, 0:96] = b2[...].astype(F32)
    share = [b2_wide[pl.ds(core * 2 + e, 8, stride=4), :] for e in range(2)]
    share = jnp.concatenate(share, axis=0).astype(BF16)
    for peer in range(16):
        sent[peer, 192:208, :] = share
    lane = lax.broadcasted_iota(jnp.int32, (8, 128), 1) // 32
    outs = []
    for v in range(4):
        for copy in copies[v * 2 : v * 2 + 2]:
            copy.wait()
        trunc = nt_dot(b1t[...], cells[v].reshape(1024, 512))
        for b in range(8):
            rows[pl.ds(b, 96, stride=8), :] = trunc[:, b * 128 : (b + 1) * 128]
        for block in range(24):
            first = block * 32
            part = [rows[first + rr * 8 : first + rr * 8 + 8, :] for rr in range(4)]
            for jj in range(4):
                moved = [
                    part[rr] if rr == jj else pltpu.roll(part[rr], (32 * (rr - jj)) % 128, 1)
                    for rr in range(4)
                ]
                low = jnp.where(lane == 0, moved[0], moved[1])
                high = jnp.where(lane == 2, moved[2], moved[3])
                tiles[first + jj * 8 : first + jj * 8 + 8, :] = jnp.where(lane < 2, low, high)
        block = slice(v * 4, v * 4 + 4)
        sent[block, 0:192, :] = tiles[...].astype(BF16).reshape(4, 192, 128)
        outs.append(pltpu.make_async_copy(sent.at[block], out_ref.at[block], sems.at[10 + v]))
        outs[-1].start()
    for copy in outs:
        copy.wait()


truncate = call(
    truncate_kernel,
    shape((16, 208, 128)),
    [
        pltpu.VMEM((96, 512), BF16),
        pltpu.VMEM((32, 96), BF16),
        pltpu.VMEM((32, 128), F32),
        pltpu.VMEM((4, 32, 32, 512), BF16),
        pltpu.VMEM((768, 128), F32),
        pltpu.VMEM((768, 128), F32),
        pltpu.VMEM((16, 208, 128), BF16),
        pltpu.SemaphoreType.DMA((14,)),
    ],
    [HBM, HBM, HBM],
    WIDE,
    HBM,
    "truncate",
)


def split_kernel(one_ref, other_ref, own_ref, gram):
    core = lax.axis_index("gz") % 2
    for c in range(4):
        gram[c * 512 : (c + 1) * 512, :] = one_ref[:, c * 128 : (c + 1) * 128]
    for out_ref, side in ((other_ref, 1 - core), (own_ref, core)):
        for b in range(8):
            for c in range(4):
                for e in range(2):
                    at = c * 32 + e * 16
                    rows = gram[pl.ds(c * 512 + b * 4 + side * 2 + e, 16, stride=32), :]
                    out_ref[b // 2, b % 2, at : at + 16, :] = rows.astype(BF16)


split = call(
    split_kernel,
    (shape((4, 2, 128, 128)), shape((4, 2, 128, 128))),
    [pltpu.VMEM((2048, 128), F32)],
    name="split",
)


def along_y_kernel(own_ref, got_ref, *out_refs):
    y = lax.axis_index("gz") // 4
    for distance, out_ref in enumerate(out_refs):
        at = lax.rem(y + distance, 4)
        out_ref[...] = (own_ref[at].astype(F32) + got_ref[at].astype(F32)).astype(BF16)


along_y = call(along_y_kernel, tuple(shape((2, 128, 128)) for _ in range(4)), name="along_y")


def along_z_kernel(*refs):
    other_ref, own_ref = refs[4:]
    place = lax.axis_index("gz") // 2 % 2
    for out_ref, at in ((other_ref, 1 - place), (own_ref, place)):
        total = refs[0][at].astype(F32)
        for ref in refs[1:4]:
            total = total + ref[at].astype(F32)
        out_ref[...] = total.astype(BF16)


along_z = call(along_z_kernel, (shape((128, 128)), shape((128, 128))), name="along_z")


def gram_kernel(away, whole_ref, *refs):
    out_ref, gram = refs[-2:]
    side = (lax.axis_index("gz") + away) % 2

    def cells(first, size):
        parts = [whole_ref[:, pl.ds(a * 32 + first, size), :] for a in range(6)]
        return jnp.concatenate([part.reshape(16 * size, 128) for part in parts], axis=1)

    values = nt_dot(cells(pl.multiple_of(side * 16, 16), 16), cells(0, 32))
    for c in range(4):
        gram[c * 256 : (c + 1) * 256, :] = values[:, c * 128 : (c + 1) * 128]
    for b in range(8):
        for c in range(4):
            rows = gram[pl.ds(c * 256 + b, 32, stride=8), :]
            out_ref[b, c * 32 : c * 32 + 32, :] = rows.astype(BF16)


def gram_part(away, whole, *after):
    return call(
        functools.partial(gram_kernel, away),
        shape((8, 128, 128)),
        [pltpu.VMEM((1024, 128), F32)],
        [VMEM] + [ANY] * len(after),
        name="gram_other" if away else "gram_own",
    )(whole, *after)


def core_rows(parts_ref, b, side):
    pieces = []
    for t in range(6):
        at = pl.multiple_of((side + b * 2) * 48 + t * 8, 8)
        pieces += [parts_ref[a, pl.ds(at, 8), :] for a in range(3)]
    rest = jnp.concatenate(pieces[14:], axis=0)
    rest = [pltpu.roll(rest, 96 - 32 * g, 1) for g in range(3)]
    rest = jnp.concatenate(rest + [jnp.zeros((16, 128), F32)], axis=0)
    lane = lax.broadcasted_iota(jnp.int32, (112, 128), 1)
    return jnp.where(lane < 96, jnp.concatenate(pieces[:14], axis=0), rest)


def core_kernel(whole_ref, got_ref, kron_ref, after_ref, other_ref, parts_ref, basis):
    core = lax.axis_index("gz") % 2
    basis[:, core] = whole_ref[:, 192:208, :]
    basis[:, 1 - core] = got_ref[...]
    x = [whole_ref[:, a * 32 : (a + 1) * 32, :].reshape(512, 128) for a in range(6)]
    mixed = lax.dot_general(
        basis[...].reshape(512, 128),
        jnp.concatenate(x, axis=1),
        (((0,), (0,)), ((), ())),
        preferred_element_type=F32,
    )
    high = mixed.astype(BF16)
    low = (mixed - high.astype(F32)).astype(BF16)
    for a in range(3):
        lanes = slice(a * 256, (a + 1) * 256)
        parts_ref[a] = nt_dot(kron_ref[...], high[:, lanes]) + nt_dot(kron_ref[...], low[:, lanes])
    for b in range(8):
        other_ref[b] = core_rows(parts_ref, b, 1 - core).astype(BF16)


core_part = call(
    core_kernel,
    (shape((8, 112, 128)), shape((3, 768, 128), F32)),
    [pltpu.VMEM((16, 2, 16, 128), BF16)],
    [VMEM, VMEM, VMEM, ANY],
    name="core_part",
)


def pair_kernel(gram_ref, gram_got_ref, parts_ref, core_got_ref, out_ref):
    core = lax.axis_index("gz") % 2
    out_ref[:, 0:128, :] = (gram_ref[...].astype(F32) + gram_got_ref[...].astype(F32)).astype(BF16)
    for b in range(8):
        total = core_rows(parts_ref, b, core) + core_got_ref[b].astype(F32)
        out_ref[b, 128:240, :] = total.astype(BF16)


pair = call(pair_kernel, shape((8, 240, 128)), name="pair")


def middle_kernel(in_ref, one_ref, one_got_ref, out_ref, sums, core, cut):
    total = in_ref[0].astype(F32)
    for source in range(1, 8):
        total = total + in_ref[source].astype(F32)
    sums[...] = total[0:128]
    cut[...] = jnp.zeros_like(cut)
    one = one_ref[...].astype(F32) + one_got_ref[...].astype(F32)
    for c in range(4):
        for e in range(2):
            at = c * 32 + e * 16
            cut[pl.ds(e * 4 + c, 16, stride=32), :] = one[at : at + 16]
            cut[pl.ds(8 + e * 4 + c, 16, stride=32), :] = sums[pl.ds(c * 32 + e, 16, stride=2), :]
    rest = [pltpu.roll(total[128 + g * 32 : 160 + g * 32], (32 + 32 * g) % 128, 1) for g in range(3)]
    lane = lax.broadcasted_iota(jnp.int32, (32, 128), 1)
    rest = jnp.where(lane < 32, rest[0], jnp.where(lane < 64, rest[1], rest[2]))
    core[0:128, :] = jnp.concatenate([total[128:240], rest[0:16]], axis=0).T
    tail = jnp.concatenate([rest[16:32], jnp.zeros((112, 128), F32)], axis=0)
    core[128:256, :] = tail.T
    for s in range(6):
        cut[pl.ds(16 + s, 16, stride=32), :] = core[pl.ds(s, 16, stride=6), :]
        cut[pl.ds(22 + s, 16, stride=32), :] = core[pl.ds(128 + s, 16, stride=6), :]
    out_ref[...] = cut[...].astype(BF16).reshape(16, 32, 128)


middle = call(
    middle_kernel,
    shape((16, 32, 128)),
    [pltpu.VMEM((128, 128), F32), pltpu.VMEM((256, 128), F32), pltpu.VMEM((512, 128), F32)],
    name="middle",
)


def last_kernel(scale_one, scale_two, in_ref, one_ref, two_ref, core_ref, turned, ordered, core):
    total = in_ref[0, 0:16, :].astype(F32)
    for source in range(1, 16):
        total = total + in_ref[source, 0:16, :].astype(F32)
    turned[...] = jnp.concatenate([total[8:16], jnp.zeros((120, 128), F32)], axis=0).T
    for group in range(4):
        for jj in range(4):
            rows = turned[group * 32 + jj * 8 : group * 32 + jj * 8 + 8, :]
            ordered[pl.ds(group * 32 + jj, 8, stride=4), :] = rows
    two = ordered[...].T
    for e in range(2):
        for c in range(4):
            lanes = slice(c * 128, (c + 1) * 128)
            one_ref[e : e + 1, lanes] = total[e * 4 + c : e * 4 + c + 1] * scale_one
            two_ref[e : e + 1, lanes] = two[e * 4 + c : e * 4 + c + 1] * scale_two
    lane = lax.broadcasted_iota(jnp.int32, (16, 128), 1)
    for v in range(4):
        blocks = [in_ref[v * 4 + g, 16:32, :].astype(F32) for g in range(4)]
        for t in range(6):
            row = jnp.zeros((16, 128), F32)
            for g in range(4):
                shift = (24 * (g - t)) % 128
                moved = pltpu.roll(blocks[g], shift, 1) if shift else blocks[g]
                if t == 5:
                    rest = jnp.concatenate([blocks[g][6:16], blocks[g][0:6]], axis=0)
                    rest = pltpu.roll(rest, 24 * g + 8, 1)
                    moved = jnp.where(lane < 24 * g + 8, moved, rest)
                row = jnp.where((lane >= 24 * g) & (lane < 24 * g + 24), moved, row)
            core[pl.ds(t * 4 + v, 8, stride=24), :] = row[0:8]
    for s in range(6):
        for t in range(6):
            core_ref[s, t] = core[(s * 6 + t) * 4 : (s * 6 + t) * 4 + 4, 0:96]


def last(received, scale_one, scale_two):
    def body(*refs):
        last_kernel(scale_one, scale_two, *refs)

    outs = (shape((2, 512), F32), shape((2, 512), F32), shape((6, 6, 4, 96), F32))
    scratch = [pltpu.VMEM((rows, 128), F32) for rows in (128, 128, 192)]
    return call(body, outs, scratch, name="last")(received)


def along_gz(y, z_lo, core):
    return [
        (i, (i // 4 + y) % 4 * 4 + (i // 2 % 2 ^ z_lo) * 2 + (i % 2 ^ core)) for i in range(16)
    ]


def send(block, y=0, z_lo=0, core=0):
    return lax.ppermute(block, "gz", along_gz(y, z_lo, core))


def shards(field, basis_one, basis_two, basis_three):
    sent = truncate(basis_one.T, basis_two, field)
    sent, field, basis_three = lax.optimization_barrier((sent, field, basis_three))
    whole = lax.all_to_all(sent, "gy", split_axis=0, concat_axis=0, tiled=True)

    flattened = field.reshape(-1, 512)
    one = jnp.dot(flattened.T, flattened, preferred_element_type=F32)
    other, own = split(one)
    blocks = along_y(own, send(other, core=1))
    blocks = [blocks[0]] + [send(blocks[d], y=d) for d in range(1, 4)]
    other, one_own = along_z(*blocks)
    one_got = send(other, z_lo=1)

    repeated = jnp.tile(basis_three.T, (1, 8))[:, None, :]
    same = jnp.arange(8)[:, None] == jnp.arange(256)[None, :] // 32
    kron = jnp.where(same[None], repeated, jnp.zeros((), BF16)).reshape(768, 256)

    basis_got = send(whole[:, 192:208], core=1)
    gram_other = gram_part(1, whole, one_own, one_got)
    gram_got = send(gram_other, core=1)
    core_other, core_parts = core_part(whole, basis_got, kron, gram_other)
    core_got = send(core_other, core=1)
    gram_own = gram_part(0, whole, core_other)
    summed = pair(gram_own, gram_got, core_parts, core_got)
    groups = [[2 * b + core for b in range(8)] for core in range(2)]
    summed = lax.all_to_all(
        summed, "gz", split_axis=0, concat_axis=0, tiled=True, axis_index_groups=groups
    )
    cut = middle(summed, one_own, one_got)
    cut = lax.all_to_all(cut, "gy", split_axis=0, concat_axis=0, tiled=True)
    gram_one, gram_two, core = last(cut, 1.0 / 1048576, 1.0 / 196608)
    return (gram_one, gram_two, jnp.transpose(core, (2, 0, 1, 3)))


def solution(mesh):
    in_specs = (P(None, "gy", "gz", None), P(), P("gy", None), P("gz", None))
    out_specs = (P(("gy", "gz"), None), P(("gy", "gz"), None), P(None, "gy", "gz", None))
    return jax.shard_map(shards, mesh=mesh, in_specs=in_specs, out_specs=out_specs, check_vma=False)
```

```python
import functools

import jax
import jax.numpy as jnp
from jax import lax
from jax.experimental import pallas as pl
from jax.experimental.pallas import tpu as pltpu
from jax.sharding import PartitionSpec as P

F32 = jnp.float32
BF16 = jnp.bfloat16
WIDE = 60 * 1024 * 1024
LIMIT = 48 * 1024 * 1024
VMEM = pl.BlockSpec(memory_space=pltpu.VMEM)
HBM = pl.BlockSpec(memory_space=pltpu.HBM)
ANY = pl.BlockSpec(memory_space=pl.ANY)


def nt_dot(a, b):
    return lax.dot_general(a, b, (((1,), (1,)), ((), ())), preferred_element_type=F32)


def call(kernel, outs, scratch=(), specs=None, limit=LIMIT, out_specs=None, name=None):
    keywords = {} if out_specs is None else {"out_specs": out_specs}
    return lambda *args: pl.pallas_call(
        kernel,
        out_shape=outs,
        in_specs=[VMEM] * len(args) if specs is None else specs,
        scratch_shapes=list(scratch),
        compiler_params=pltpu.CompilerParams(vmem_limit_bytes=limit),
        name=name,
        **keywords,
    )(*args)


def shape(dims, dtype=BF16):
    return jax.ShapeDtypeStruct(dims, dtype)


def truncate_kernel(b1t_ref, b2_ref, field_ref, out_ref, b1t, b2, b2_wide, cells, rows, tiles, sent, sems):
    core = lax.axis_index("gz") % 2
    small = [
        pltpu.make_async_copy(b1t_ref, b1t, sems.at[0]),
        pltpu.make_async_copy(b2_ref, b2, sems.at[1]),
    ]
    for copy in small:
        copy.start()
    copies = []
    for piece in range(8):
        v, half = piece // 2, pl.ds(piece % 2 * 16, 16)
        copies.append(
            pltpu.make_async_copy(field_ref.at[v, half], cells.at[v, half], sems.at[2 + piece])
        )
        copies[-1].start()
    for copy in small:
        copy.wait()
    b2_wide[...] = jnp.zeros_like(b2_wide)
    b2_wide[:, 0:96] = b2[...].astype(F32)
    share = [b2_wide[pl.ds(core * 2 + e, 8, stride=4), :] for e in range(2)]
    share = jnp.concatenate(share, axis=0).astype(BF16)
    for peer in range(16):
        sent[peer, 192:208, :] = share
    lane = lax.broadcasted_iota(jnp.int32, (8, 128), 1) // 32
    outs = []
    for v in range(4):
        for copy in copies[v * 2 : v * 2 + 2]:
            copy.wait()
        trunc = nt_dot(b1t[...], cells[v].reshape(1024, 512))
        for b in range(8):
            rows[pl.ds(b, 96, stride=8), :] = trunc[:, b * 128 : (b + 1) * 128]
        for block in range(24):
            first = block * 32
            part = [rows[first + rr * 8 : first + rr * 8 + 8, :] for rr in range(4)]
            for jj in range(4):
                moved = [
                    part[rr] if rr == jj else pltpu.roll(part[rr], (32 * (rr - jj)) % 128, 1)
                    for rr in range(4)
                ]
                low = jnp.where(lane == 0, moved[0], moved[1])
                high = jnp.where(lane == 2, moved[2], moved[3])
                tiles[first + jj * 8 : first + jj * 8 + 8, :] = jnp.where(lane < 2, low, high)
        block = slice(v * 4, v * 4 + 4)
        sent[block, 0:192, :] = tiles[...].astype(BF16).reshape(4, 192, 128)
        outs.append(pltpu.make_async_copy(sent.at[block], out_ref.at[block], sems.at[10 + v]))
        outs[-1].start()
    for copy in outs:
        copy.wait()


truncate = call(
    truncate_kernel,
    shape((16, 208, 128)),
    [
        pltpu.VMEM((96, 512), BF16),
        pltpu.VMEM((32, 96), BF16),
        pltpu.VMEM((32, 128), F32),
        pltpu.VMEM((4, 32, 32, 512), BF16),
        pltpu.VMEM((768, 128), F32),
        pltpu.VMEM((768, 128), F32),
        pltpu.VMEM((16, 208, 128), BF16),
        pltpu.SemaphoreType.DMA((14,)),
    ],
    [HBM, HBM, HBM],
    WIDE,
    HBM,
    "truncate",
)


def split_kernel(one_ref, other_ref, own_ref, gram):
    core = lax.axis_index("gz") % 2
    for c in range(4):
        gram[c * 512 : (c + 1) * 512, :] = one_ref[:, c * 128 : (c + 1) * 128]
    for out_ref, side in ((other_ref, 1 - core), (own_ref, core)):
        for b in range(8):
            for c in range(4):
                for e in range(2):
                    at = c * 32 + e * 16
                    rows = gram[pl.ds(c * 512 + b * 4 + side * 2 + e, 16, stride=32), :]
                    out_ref[b // 2, b % 2, at : at + 16, :] = rows.astype(BF16)


split = call(
    split_kernel,
    (shape((4, 2, 128, 128)), shape((4, 2, 128, 128))),
    [pltpu.VMEM((2048, 128), F32)],
    name="split",
)


def along_y_kernel(own_ref, got_ref, *out_refs):
    y = lax.axis_index("gz") // 4
    for distance, out_ref in enumerate(out_refs):
        at = lax.rem(y + distance, 4)
        out_ref[...] = (own_ref[at].astype(F32) + got_ref[at].astype(F32)).astype(BF16)


along_y = call(along_y_kernel, tuple(shape((2, 128, 128)) for _ in range(4)), name="along_y")


def along_z_kernel(*refs):
    other_ref, own_ref = refs[4:]
    place = lax.axis_index("gz") // 2 % 2
    for out_ref, at in ((other_ref, 1 - place), (own_ref, place)):
        total = refs[0][at].astype(F32)
        for ref in refs[1:4]:
            total = total + ref[at].astype(F32)
        out_ref[...] = total.astype(BF16)


along_z = call(along_z_kernel, (shape((128, 128)), shape((128, 128))), name="along_z")


def gram_rows(whole_ref, side, out_ref, gram):
    def cells(first, size):
        parts = [whole_ref[:, pl.ds(a * 32 + first, size), :] for a in range(6)]
        return jnp.concatenate([part.reshape(16 * size, 128) for part in parts], axis=1)

    values = nt_dot(cells(pl.multiple_of(side * 16, 16), 16), cells(0, 32))
    for c in range(4):
        gram[c * 256 : (c + 1) * 256, :] = values[:, c * 128 : (c + 1) * 128]
    for b in range(8):
        for c in range(4):
            rows = gram[pl.ds(c * 256 + b, 32, stride=8), :]
            out_ref[b, c * 32 : c * 32 + 32, :] = rows.astype(BF16)


def core_rows(kron_ref, high_ref, low_ref, side, out_ref):
    kron = kron_ref[pl.ds(pl.multiple_of(side * 384, 384), 384), :]
    parts = []
    for a in range(3):
        lanes = slice(a * 256, (a + 1) * 256)
        parts.append(nt_dot(kron, high_ref[:, lanes]) + nt_dot(kron, low_ref[:, lanes]))
    lane = lax.broadcasted_iota(jnp.int32, (112, 128), 1)
    for b in range(8):
        pieces = []
        for t in range(6):
            at = b * 48 + t * 8
            pieces += [part[at : at + 8] for part in parts]
        rest = jnp.concatenate(pieces[14:], axis=0)
        rest = [pltpu.roll(rest, 96 - 32 * g, 1) for g in range(3)]
        rest = jnp.concatenate(rest + [jnp.zeros((16, 128), F32)], axis=0)
        packed = jnp.where(lane < 96, jnp.concatenate(pieces[:14], axis=0), rest)
        out_ref[b] = packed.astype(out_ref.dtype)


def gram_kernel(whole_ref, after_ref, out_ref, gram):
    gram_rows(whole_ref, 1 - lax.axis_index("gz") % 2, out_ref, gram)


gram_part = call(
    gram_kernel,
    shape((8, 128, 128)),
    [pltpu.VMEM((1024, 128), F32)],
    [VMEM, ANY],
    name="gram_other",
)


def core_kernel(whole_ref, got_ref, kron_ref, *refs):
    out_ref, high_ref, low_ref, basis = refs[-4:]
    core = lax.axis_index("gz") % 2
    basis[:, core] = whole_ref[:, 192:208, :]
    basis[:, 1 - core] = got_ref[...]
    x = [whole_ref[:, a * 32 : (a + 1) * 32, :].reshape(512, 128) for a in range(6)]
    mixed = lax.dot_general(
        basis[...].reshape(512, 128),
        jnp.concatenate(x, axis=1),
        (((0,), (0,)), ((), ())),
        preferred_element_type=F32,
    )
    high_ref[...] = mixed.astype(BF16)
    low_ref[...] = (mixed - high_ref[...].astype(F32)).astype(BF16)
    core_rows(kron_ref, high_ref, low_ref, 1 - core, out_ref)


core_part = call(
    core_kernel,
    (shape((8, 112, 128)), shape((128, 768)), shape((128, 768))),
    [pltpu.VMEM((16, 2, 16, 128), BF16)],
    [VMEM, VMEM, VMEM, ANY, ANY],
    name="core_other",
)


def own_kernel(whole_ref, kron_ref, high_ref, low_ref, after_ref, gram_ref, core_ref, gram):
    core = lax.axis_index("gz") % 2
    gram_rows(whole_ref, core, gram_ref, gram)
    core_rows(kron_ref, high_ref, low_ref, core, core_ref)


own_part = call(
    own_kernel,
    (shape((8, 128, 128)), shape((8, 112, 128), F32)),
    [pltpu.VMEM((1024, 128), F32)],
    [VMEM] * 4 + [ANY],
    name="own",
)


def pair_kernel(gram_ref, gram_got_ref, core_ref, core_got_ref, out_ref):
    out_ref[:, 0:128, :] = (gram_ref[...].astype(F32) + gram_got_ref[...].astype(F32)).astype(BF16)
    out_ref[:, 128:240, :] = (core_ref[...] + core_got_ref[...].astype(F32)).astype(BF16)


pair = call(pair_kernel, shape((8, 240, 128)), name="pair")


def middle_kernel(in_ref, one_ref, one_got_ref, out_ref, sums, core, cut):
    total = in_ref[0].astype(F32)
    for source in range(1, 8):
        total = total + in_ref[source].astype(F32)
    sums[...] = total[0:128]
    cut[...] = jnp.zeros_like(cut)
    one = one_ref[...].astype(F32) + one_got_ref[...].astype(F32)
    for c in range(4):
        for e in range(2):
            at = c * 32 + e * 16
            cut[pl.ds(e * 4 + c, 16, stride=24), :] = one[at : at + 16]
            cut[pl.ds(8 + e * 4 + c, 16, stride=24), :] = sums[pl.ds(c * 32 + e, 16, stride=2), :]
    rest = [pltpu.roll(total[128 + g * 32 : 160 + g * 32], (32 + 32 * g) % 128, 1) for g in range(3)]
    lane = lax.broadcasted_iota(jnp.int32, (32, 128), 1)
    rest = jnp.where(lane < 32, rest[0], jnp.where(lane < 64, rest[1], rest[2]))
    core[0:128, :] = jnp.concatenate([total[128:240], rest[0:16]], axis=0).T
    tail = jnp.concatenate([rest[16:32], jnp.zeros((112, 128), F32)], axis=0)
    core[128:256, :] = tail.T
    lane = lax.broadcasted_iota(jnp.int32, (16, 128), 1) // 16
    last = jnp.zeros((16, 128), F32)
    for s in range(6):
        cut[pl.ds(16 + s, 16, stride=24), :] = core[pl.ds(s, 16, stride=6), :]
        part = core[pl.ds(128 + s, 16, stride=6), :]
        last = jnp.where(lane == s, pltpu.roll(part, 16 * s, 1) if s else part, last)
    cut[pl.ds(22, 16, stride=24), :] = last
    out_ref[...] = cut[...].reshape(16, 24, 128).astype(BF16)


middle = call(
    middle_kernel,
    shape((16, 24, 128)),
    [pltpu.VMEM((128, 128), F32), pltpu.VMEM((256, 128), F32), pltpu.VMEM((384, 128), F32)],
    name="middle",
)


def last_kernel(scale_one, scale_two, in_ref, one_ref, two_ref, core_ref, turned, ordered, core):
    got = in_ref[...].astype(F32)
    total = got[0, 0:16]
    for source in range(1, 16):
        total = total + got[source, 0:16]
    turned[...] = jnp.concatenate([total[8:16], jnp.zeros((120, 128), F32)], axis=0).T
    for group in range(4):
        for jj in range(4):
            rows = turned[group * 32 + jj * 8 : group * 32 + jj * 8 + 8, :]
            ordered[pl.ds(group * 32 + jj, 8, stride=4), :] = rows
    two = ordered[...].T
    for e in range(2):
        for c in range(4):
            lanes = slice(c * 128, (c + 1) * 128)
            one_ref[e : e + 1, lanes] = total[e * 4 + c : e * 4 + c + 1] * scale_one
            two_ref[e : e + 1, lanes] = two[e * 4 + c : e * 4 + c + 1] * scale_two
    lane = lax.broadcasted_iota(jnp.int32, (8, 128), 1)
    row = lax.broadcasted_iota(jnp.int32, (8, 128), 0)
    for v in range(4):
        blocks = [got[v * 4 + g, 16:24] for g in range(4)]
        for t in range(6):
            ranks = jnp.zeros((8, 128), F32)
            for g in range(4):
                shift = (24 * (g - t)) % 128
                moved = pltpu.roll(blocks[g], shift, 1) if shift else blocks[g]
                if t == 5:
                    rest = jnp.zeros((8, 128), F32)
                    for s in range(6):
                        turned = pltpu.roll(blocks[g], (24 * g + 8 - 16 * s) % 128, 1)
                        rest = jnp.where(row == s, turned[6:7], rest)
                    moved = jnp.where(lane < 24 * g + 8, moved, rest)
                ranks = jnp.where((lane >= 24 * g) & (lane < 24 * g + 24), moved, ranks)
            core[pl.ds(t * 4 + v, 8, stride=24), :] = ranks
    for s in range(6):
        for t in range(6):
            core_ref[s, t] = core[(s * 6 + t) * 4 : (s * 6 + t) * 4 + 4, 0:96]


def last(received, scale_one, scale_two):
    def body(*refs):
        last_kernel(scale_one, scale_two, *refs)

    outs = (shape((2, 512), F32), shape((2, 512), F32), shape((6, 6, 4, 96), F32))
    scratch = [pltpu.VMEM((rows, 128), F32) for rows in (128, 128, 192)]
    return call(body, outs, scratch, name="last")(received)


def along_gz(y, z_lo, core):
    return [
        (i, (i // 4 + y) % 4 * 4 + (i // 2 % 2 ^ z_lo) * 2 + (i % 2 ^ core)) for i in range(16)
    ]


def send(block, y=0, z_lo=0, core=0):
    return lax.ppermute(block, "gz", along_gz(y, z_lo, core))


def shards(field, basis_one, basis_two, basis_three):
    sent = truncate(basis_one.T, basis_two, field)
    sent, field, basis_three = lax.optimization_barrier((sent, field, basis_three))
    whole = lax.all_to_all(sent, "gy", split_axis=0, concat_axis=0, tiled=True)

    flattened = field.reshape(-1, 512)
    one = jnp.dot(flattened.T, flattened, preferred_element_type=F32)
    other, own = split(one)
    blocks = along_y(own, send(other, core=1))
    blocks = [blocks[0]] + [send(blocks[d], y=d) for d in range(1, 4)]
    other, one_own = along_z(*blocks)
    one_got = send(other, z_lo=1)

    turned = jnp.transpose(basis_three.reshape(32, 8, 2, 6), (2, 1, 3, 0)).reshape(96, 32)
    repeated = jnp.tile(turned, (1, 8))[:, None, :]
    same = jnp.arange(8)[:, None] == jnp.arange(256)[None, :] // 32
    kron = jnp.where(same[None], repeated, jnp.zeros((), BF16)).reshape(768, 256)

    basis_got = send(whole[:, 192:208], core=1)
    gram_other = gram_part(whole, one_own)
    gram_got = send(gram_other, core=1)
    core_other, high, low = core_part(whole, basis_got, kron, gram_other, one_got)
    core_got = send(core_other, core=1)
    gram_own, core_own = own_part(whole, kron, high, low, core_other)
    summed = pair(gram_own, gram_got, core_own, core_got)
    groups = [[2 * b + core for b in range(8)] for core in range(2)]
    summed = lax.all_to_all(
        summed, "gz", split_axis=0, concat_axis=0, tiled=True, axis_index_groups=groups
    )
    cut = middle(summed, one_own, one_got)
    cut = lax.all_to_all(cut, "gy", split_axis=0, concat_axis=0, tiled=True)
    gram_one, gram_two, core = last(cut, 1.0 / 1048576, 1.0 / 196608)
    return (gram_one, gram_two, jnp.transpose(core, (2, 0, 1, 3)))


def solution(mesh):
    in_specs = (P(None, "gy", "gz", None), P(), P("gy", None), P("gz", None))
    out_specs = (P(("gy", "gz"), None), P(("gy", "gz"), None), P(None, "gy", "gz", None))
    return jax.shard_map(shards, mesh=mesh, in_specs=in_specs, out_specs=out_specs, check_vma=False)
```

```python
import functools

import jax
import jax.numpy as jnp
from jax import lax
from jax.experimental import pallas as pl
from jax.experimental.pallas import tpu as pltpu
from jax.sharding import PartitionSpec as P

F32 = jnp.float32
BF16 = jnp.bfloat16
WIDE = 60 * 1024 * 1024
LIMIT = 48 * 1024 * 1024
VMEM = pl.BlockSpec(memory_space=pltpu.VMEM)
HBM = pl.BlockSpec(memory_space=pltpu.HBM)
ANY = pl.BlockSpec(memory_space=pl.ANY)


def nt_dot(a, b):
    return lax.dot_general(a, b, (((1,), (1,)), ((), ())), preferred_element_type=F32)


def call(kernel, outs, scratch=(), specs=None, limit=LIMIT, out_specs=None, name=None):
    keywords = {} if out_specs is None else {"out_specs": out_specs}
    return lambda *args: pl.pallas_call(
        kernel,
        out_shape=outs,
        in_specs=[VMEM] * len(args) if specs is None else specs,
        scratch_shapes=list(scratch),
        compiler_params=pltpu.CompilerParams(vmem_limit_bytes=limit),
        name=name,
        **keywords,
    )(*args)


def shape(dims, dtype=BF16):
    return jax.ShapeDtypeStruct(dims, dtype)


def truncate_kernel(b1t_ref, b2_ref, field_ref, out_ref, *scratch):
    b1t, b2, b2_wide, cells, *work, sent, sems = scratch
    core = lax.axis_index("gz") % 2
    small = [
        pltpu.make_async_copy(b1t_ref, b1t, sems.at[0]),
        pltpu.make_async_copy(b2_ref, b2, sems.at[1]),
    ]
    copies = [pltpu.make_async_copy(field_ref.at[v], cells.at[v], sems.at[2 + v]) for v in range(4)]
    for copy in small + copies:
        copy.start()
    for copy in small:
        copy.wait()
    b2_wide[...] = jnp.zeros_like(b2_wide)
    b2_wide[:, 0:96] = b2[...].astype(F32)
    share = [b2_wide[pl.ds(core * 2 + e, 8, stride=4), :] for e in range(2)]
    share = jnp.concatenate(share, axis=0).astype(BF16)
    for peer in range(16):
        sent[peer, 192:208, :] = share
    lane = lax.broadcasted_iota(jnp.int32, (8, 128), 1) // 32

    def product(v):
        rows = work[v % 2]
        trunc = nt_dot(b1t[...], cells[v].reshape(1024, 512))
        for b in range(8):
            rows[pl.ds(b, 96, stride=8), :] = trunc[:, b * 128 : (b + 1) * 128]

    def arrange(v):
        rows, tiles = work[v % 2], work[2 + v % 2]
        for block in range(24):
            first = block * 32
            part = [rows[first + rr * 8 : first + rr * 8 + 8, :] for rr in range(4)]
            for jj in range(4):
                moved = [
                    part[rr] if rr == jj else pltpu.roll(part[rr], (32 * (rr - jj)) % 128, 1)
                    for rr in range(4)
                ]
                low = jnp.where(lane == 0, moved[0], moved[1])
                high = jnp.where(lane == 2, moved[2], moved[3])
                tiles[first + jj * 8 : first + jj * 8 + 8, :] = jnp.where(lane < 2, low, high)
        sent[v * 4 : v * 4 + 4, 0:192, :] = tiles[...].astype(BF16).reshape(4, 192, 128)

    outs = []
    for v in range(5):
        if v < 4:
            copies[v].wait()
            product(v)
        if v > 0:
            arrange(v - 1)
            block = slice(v * 4 - 4, v * 4)
            outs.append(pltpu.make_async_copy(sent.at[block], out_ref.at[block], sems.at[5 + v]))
            outs[-1].start()
    for copy in outs:
        copy.wait()


truncate = call(
    truncate_kernel,
    shape((16, 208, 128)),
    [
        pltpu.VMEM((96, 512), BF16),
        pltpu.VMEM((32, 96), BF16),
        pltpu.VMEM((32, 128), F32),
        pltpu.VMEM((4, 32, 32, 512), BF16),
        *[pltpu.VMEM((768, 128), F32)] * 4,
        pltpu.VMEM((16, 208, 128), BF16),
        pltpu.SemaphoreType.DMA((10,)),
    ],
    [HBM, HBM, HBM],
    WIDE,
    HBM,
    "truncate",
)


def split_kernel(one_ref, other_ref, own_ref, gram):
    core = lax.axis_index("gz") % 2
    for c in range(4):
        gram[c * 512 : (c + 1) * 512, :] = one_ref[:, c * 128 : (c + 1) * 128]
    for out_ref, side in ((other_ref, 1 - core), (own_ref, core)):
        for b in range(8):
            for c in range(4):
                for e in range(2):
                    at = c * 32 + e * 16
                    rows = gram[pl.ds(c * 512 + b * 4 + side * 2 + e, 16, stride=32), :]
                    out_ref[b // 2, b % 2, at : at + 16, :] = rows.astype(BF16)


split = call(
    split_kernel,
    (shape((4, 2, 128, 128)), shape((4, 2, 128, 128))),
    [pltpu.VMEM((2048, 128), F32)],
    name="split",
)


def along_y_kernel(own_ref, got_ref, *out_refs):
    y = lax.axis_index("gz") // 4
    for distance, out_ref in enumerate(out_refs):
        at = lax.rem(y + distance, 4)
        out_ref[...] = (own_ref[at].astype(F32) + got_ref[at].astype(F32)).astype(BF16)


along_y = call(along_y_kernel, tuple(shape((2, 128, 128)) for _ in range(4)), name="along_y")


def along_z_kernel(*refs):
    other_ref, own_ref = refs[4:]
    place = lax.axis_index("gz") // 2 % 2
    for out_ref, at in ((other_ref, 1 - place), (own_ref, place)):
        total = refs[0][at].astype(F32)
        for ref in refs[1:4]:
            total = total + ref[at].astype(F32)
        out_ref[...] = total.astype(BF16)


along_z = call(along_z_kernel, (shape((128, 128)), shape((128, 128))), name="along_z")


def gram_rows(whole_ref, side, out_ref, gram):
    def cells(first, size):
        parts = [whole_ref[:, pl.ds(a * 32 + first, size), :] for a in range(6)]
        return jnp.concatenate([part.reshape(16 * size, 128) for part in parts], axis=1)

    values = nt_dot(cells(pl.multiple_of(side * 16, 16), 16), cells(0, 32))
    for c in range(4):
        gram[c * 256 : (c + 1) * 256, :] = values[:, c * 128 : (c + 1) * 128]
    for b in range(8):
        for c in range(4):
            rows = gram[pl.ds(c * 256 + b, 32, stride=8), :]
            out_ref[b, c * 32 : c * 32 + 32, :] = rows.astype(BF16)


def core_rows(kron_ref, high_ref, low_ref, side, out_ref):
    kron = kron_ref[pl.ds(pl.multiple_of(side * 384, 384), 384), :]
    parts = []
    for a in range(3):
        lanes = slice(a * 256, (a + 1) * 256)
        parts.append(nt_dot(kron, high_ref[:, lanes]) + nt_dot(kron, low_ref[:, lanes]))
    lane = lax.broadcasted_iota(jnp.int32, (112, 128), 1)
    for b in range(8):
        pieces = []
        for t in range(6):
            at = b * 48 + t * 8
            pieces += [part[at : at + 8] for part in parts]
        rest = jnp.concatenate(pieces[14:], axis=0)
        rest = [pltpu.roll(rest, 96 - 32 * g, 1) for g in range(3)]
        rest = jnp.concatenate(rest + [jnp.zeros((16, 128), F32)], axis=0)
        packed = jnp.where(lane < 96, jnp.concatenate(pieces[:14], axis=0), rest)
        out_ref[b] = packed.astype(out_ref.dtype)


def gram_kernel(whole_ref, after_ref, out_ref, gram):
    gram_rows(whole_ref, 1 - lax.axis_index("gz") % 2, out_ref, gram)


gram_part = call(
    gram_kernel,
    shape((8, 128, 128)),
    [pltpu.VMEM((1024, 128), F32)],
    [VMEM, ANY],
    name="gram_other",
)


def core_kernel(whole_ref, got_ref, kron_ref, *refs):
    out_ref, high_ref, low_ref, basis = refs[-4:]
    core = lax.axis_index("gz") % 2
    basis[:, core] = whole_ref[:, 192:208, :]
    basis[:, 1 - core] = got_ref[...]
    x = [whole_ref[:, a * 32 : (a + 1) * 32, :].reshape(512, 128) for a in range(6)]
    mixed = lax.dot_general(
        basis[...].reshape(512, 128),
        jnp.concatenate(x, axis=1),
        (((0,), (0,)), ((), ())),
        preferred_element_type=F32,
    )
    high_ref[...] = mixed.astype(BF16)
    low_ref[...] = (mixed - high_ref[...].astype(F32)).astype(BF16)
    core_rows(kron_ref, high_ref, low_ref, 1 - core, out_ref)


core_part = call(
    core_kernel,
    (shape((8, 112, 128)), shape((128, 768)), shape((128, 768))),
    [pltpu.VMEM((16, 2, 16, 128), BF16)],
    [VMEM, VMEM, VMEM, ANY, ANY],
    name="core_other",
)


def own_kernel(whole_ref, kron_ref, high_ref, low_ref, after_ref, gram_ref, core_ref, gram):
    core = lax.axis_index("gz") % 2
    gram_rows(whole_ref, core, gram_ref, gram)
    core_rows(kron_ref, high_ref, low_ref, core, core_ref)


own_part = call(
    own_kernel,
    (shape((8, 128, 128)), shape((8, 112, 128), F32)),
    [pltpu.VMEM((1024, 128), F32)],
    [VMEM] * 4 + [ANY],
    name="own",
)


def pair_kernel(gram_ref, gram_got_ref, core_ref, core_got_ref, out_ref):
    out_ref[:, 0:128, :] = (gram_ref[...].astype(F32) + gram_got_ref[...].astype(F32)).astype(BF16)
    out_ref[:, 128:240, :] = (core_ref[...] + core_got_ref[...].astype(F32)).astype(BF16)


pair = call(pair_kernel, shape((8, 240, 128)), name="pair")


def middle_kernel(in_ref, one_ref, one_got_ref, out_ref, sums, core, cut):
    total = in_ref[0].astype(F32)
    for source in range(1, 8):
        total = total + in_ref[source].astype(F32)
    sums[...] = total[0:128]
    cut[...] = jnp.zeros_like(cut)
    one = one_ref[...].astype(F32) + one_got_ref[...].astype(F32)
    for c in range(4):
        for e in range(2):
            at = c * 32 + e * 16
            cut[pl.ds(e * 4 + c, 16, stride=24), :] = one[at : at + 16]
            cut[pl.ds(8 + e * 4 + c, 16, stride=24), :] = sums[pl.ds(c * 32 + e, 16, stride=2), :]
    rest = [pltpu.roll(total[128 + g * 32 : 160 + g * 32], (32 + 32 * g) % 128, 1) for g in range(3)]
    lane = lax.broadcasted_iota(jnp.int32, (32, 128), 1)
    rest = jnp.where(lane < 32, rest[0], jnp.where(lane < 64, rest[1], rest[2]))
    core[0:128, :] = jnp.concatenate([total[128:240], rest[0:16]], axis=0).T
    tail = jnp.concatenate([rest[16:32], jnp.zeros((112, 128), F32)], axis=0)
    core[128:256, :] = tail.T
    lane = lax.broadcasted_iota(jnp.int32, (16, 128), 1) // 16
    last = jnp.zeros((16, 128), F32)
    for s in range(6):
        cut[pl.ds(16 + s, 16, stride=24), :] = core[pl.ds(s, 16, stride=6), :]
        part = core[pl.ds(128 + s, 16, stride=6), :]
        last = jnp.where(lane == s, pltpu.roll(part, 16 * s, 1) if s else part, last)
    cut[pl.ds(22, 16, stride=24), :] = last
    out_ref[...] = cut[...].reshape(16, 24, 128).astype(BF16)


middle = call(
    middle_kernel,
    shape((16, 24, 128)),
    [pltpu.VMEM((128, 128), F32), pltpu.VMEM((256, 128), F32), pltpu.VMEM((384, 128), F32)],
    name="middle",
)


def last_kernel(scale_one, scale_two, in_ref, one_ref, two_ref, core_ref, turned, ordered, core):
    got = in_ref[...].astype(F32)
    total = got[0, 0:16]
    for source in range(1, 16):
        total = total + got[source, 0:16]
    turned[...] = jnp.concatenate([total[8:16], jnp.zeros((120, 128), F32)], axis=0).T
    for group in range(4):
        for jj in range(4):
            rows = turned[group * 32 + jj * 8 : group * 32 + jj * 8 + 8, :]
            ordered[pl.ds(group * 32 + jj, 8, stride=4), :] = rows
    two = ordered[...].T
    for e in range(2):
        for c in range(4):
            lanes = slice(c * 128, (c + 1) * 128)
            one_ref[e : e + 1, lanes] = total[e * 4 + c : e * 4 + c + 1] * scale_one
            two_ref[e : e + 1, lanes] = two[e * 4 + c : e * 4 + c + 1] * scale_two
    lane = lax.broadcasted_iota(jnp.int32, (8, 128), 1)
    row = lax.broadcasted_iota(jnp.int32, (8, 128), 0)
    for v in range(4):
        blocks = [got[v * 4 + g, 16:24] for g in range(4)]
        for t in range(6):
            ranks = jnp.zeros((8, 128), F32)
            for g in range(4):
                shift = (24 * (g - t)) % 128
                moved = pltpu.roll(blocks[g], shift, 1) if shift else blocks[g]
                if t == 5:
                    rest = jnp.zeros((8, 128), F32)
                    for s in range(6):
                        turned = pltpu.roll(blocks[g], (24 * g + 8 - 16 * s) % 128, 1)
                        rest = jnp.where(row == s, turned[6:7], rest)
                    moved = jnp.where(lane < 24 * g + 8, moved, rest)
                ranks = jnp.where((lane >= 24 * g) & (lane < 24 * g + 24), moved, ranks)
            core[pl.ds(t * 4 + v, 8, stride=24), :] = ranks
    for s in range(6):
        for t in range(6):
            core_ref[s, t] = core[(s * 6 + t) * 4 : (s * 6 + t) * 4 + 4, 0:96]


def last(received, scale_one, scale_two):
    def body(*refs):
        last_kernel(scale_one, scale_two, *refs)

    outs = (shape((2, 512), F32), shape((2, 512), F32), shape((6, 6, 4, 96), F32))
    scratch = [pltpu.VMEM((rows, 128), F32) for rows in (128, 128, 192)]
    return call(body, outs, scratch, name="last")(received)


def along_gz(y, z_lo, core):
    return [
        (i, (i // 4 + y) % 4 * 4 + (i // 2 % 2 ^ z_lo) * 2 + (i % 2 ^ core)) for i in range(16)
    ]


def send(block, y=0, z_lo=0, core=0):
    return lax.ppermute(block, "gz", along_gz(y, z_lo, core))


def shards(field, basis_one, basis_two, basis_three):
    sent = truncate(basis_one.T, basis_two, field)
    sent, field, basis_three = lax.optimization_barrier((sent, field, basis_three))
    whole = lax.all_to_all(sent, "gy", split_axis=0, concat_axis=0, tiled=True)

    flattened = field.reshape(-1, 512)
    one = jnp.dot(flattened.T, flattened, preferred_element_type=F32)
    other, own = split(one)
    blocks = along_y(own, send(other, core=1))
    blocks = [blocks[0]] + [send(blocks[d], y=d) for d in range(1, 4)]
    other, one_own = along_z(*blocks)
    one_got = send(other, z_lo=1)

    turned = jnp.transpose(basis_three.reshape(32, 8, 2, 6), (2, 1, 3, 0)).reshape(96, 32)
    repeated = jnp.tile(turned, (1, 8))[:, None, :]
    same = jnp.arange(8)[:, None] == jnp.arange(256)[None, :] // 32
    kron = jnp.where(same[None], repeated, jnp.zeros((), BF16)).reshape(768, 256)

    basis_got = send(whole[:, 192:208], core=1)
    gram_other = gram_part(whole, one_own)
    gram_got = send(gram_other, core=1)
    core_other, high, low = core_part(whole, basis_got, kron, gram_other, one_got)
    core_got = send(core_other, core=1)
    gram_own, core_own = own_part(whole, kron, high, low, core_other)
    summed = pair(gram_own, gram_got, core_own, core_got)
    groups = [[2 * b + core for b in range(8)] for core in range(2)]
    summed = lax.all_to_all(
        summed, "gz", split_axis=0, concat_axis=0, tiled=True, axis_index_groups=groups
    )
    cut = middle(summed, one_own, one_got)
    cut = lax.all_to_all(cut, "gy", split_axis=0, concat_axis=0, tiled=True)
    gram_one, gram_two, core = last(cut, 1.0 / 1048576, 1.0 / 196608)
    return (gram_one, gram_two, jnp.transpose(core, (2, 0, 1, 3)))


def solution(mesh):
    in_specs = (P(None, "gy", "gz", None), P(), P("gy", None), P("gz", None))
    out_specs = (P(("gy", "gz"), None), P(("gy", "gz"), None), P(None, "gy", "gz", None))
    return jax.shard_map(shards, mesh=mesh, in_specs=in_specs, out_specs=out_specs, check_vma=False)
```

```python
import functools

import jax
import jax.numpy as jnp
from jax import lax
from jax.experimental import pallas as pl
from jax.experimental.pallas import tpu as pltpu
from jax.sharding import PartitionSpec as P

F32 = jnp.float32
BF16 = jnp.bfloat16
WIDE = 60 * 1024 * 1024
LIMIT = 48 * 1024 * 1024
VMEM = pl.BlockSpec(memory_space=pltpu.VMEM)
HBM = pl.BlockSpec(memory_space=pltpu.HBM)
ANY = pl.BlockSpec(memory_space=pl.ANY)


def nt_dot(a, b):
    return lax.dot_general(a, b, (((1,), (1,)), ((), ())), preferred_element_type=F32)


def call(kernel, outs, scratch=(), specs=None, limit=LIMIT, out_specs=None, name=None):
    keywords = {} if out_specs is None else {"out_specs": out_specs}
    return lambda *args: pl.pallas_call(
        kernel,
        out_shape=outs,
        in_specs=[VMEM] * len(args) if specs is None else specs,
        scratch_shapes=list(scratch),
        compiler_params=pltpu.CompilerParams(vmem_limit_bytes=limit),
        name=name,
        **keywords,
    )(*args)


def shape(dims, dtype=BF16):
    return jax.ShapeDtypeStruct(dims, dtype)


def truncate_kernel(b1t_ref, b2_ref, field_ref, out_ref, *scratch):
    b1t, b2, b2_wide, cells, *work, sent, sems = scratch
    core = lax.axis_index("gz") % 2
    small = [
        pltpu.make_async_copy(b1t_ref, b1t, sems.at[0]),
        pltpu.make_async_copy(b2_ref, b2, sems.at[1]),
    ]
    copies = [pltpu.make_async_copy(field_ref.at[v], cells.at[v], sems.at[2 + v]) for v in range(4)]
    for copy in small + copies:
        copy.start()
    for copy in small:
        copy.wait()
    b2_wide[...] = jnp.zeros_like(b2_wide)
    b2_wide[:, 0:96] = b2[...].astype(F32)
    share = [b2_wide[pl.ds(core * 2 + e, 8, stride=4), :] for e in range(2)]
    share = jnp.concatenate(share, axis=0).astype(BF16)
    for peer in range(16):
        sent[peer, 192:208, :] = share
    lane = lax.broadcasted_iota(jnp.int32, (8, 128), 1) // 32

    def product(v):
        rows = work[v % 2]
        trunc = nt_dot(b1t[...], cells[v].reshape(1024, 512))
        for b in range(8):
            rows[pl.ds(b, 96, stride=8), :] = trunc[:, b * 128 : (b + 1) * 128]

    def arrange(v):
        rows, tiles = work[v % 2], work[2 + v % 2]
        for block in range(24):
            first = block * 32
            part = [rows[first + rr * 8 : first + rr * 8 + 8, :] for rr in range(4)]
            for jj in range(4):
                moved = [
                    part[rr] if rr == jj else pltpu.roll(part[rr], (32 * (rr - jj)) % 128, 1)
                    for rr in range(4)
                ]
                low = jnp.where(lane == 0, moved[0], moved[1])
                high = jnp.where(lane == 2, moved[2], moved[3])
                tiles[first + jj * 8 : first + jj * 8 + 8, :] = jnp.where(lane < 2, low, high)
        sent[v * 4 : v * 4 + 4, 0:192, :] = tiles[...].astype(BF16).reshape(4, 192, 128)

    outs = []
    for v in range(5):
        if v < 4:
            copies[v].wait()
            product(v)
        if v > 0:
            arrange(v - 1)
            block = slice(v * 4 - 4, v * 4)
            outs.append(pltpu.make_async_copy(sent.at[block], out_ref.at[block], sems.at[5 + v]))
            outs[-1].start()
    for copy in outs:
        copy.wait()


truncate = call(
    truncate_kernel,
    shape((16, 208, 128)),
    [
        pltpu.VMEM((96, 512), BF16),
        pltpu.VMEM((32, 96), BF16),
        pltpu.VMEM((32, 128), F32),
        pltpu.VMEM((4, 32, 32, 512), BF16),
        *[pltpu.VMEM((768, 128), F32)] * 4,
        pltpu.VMEM((16, 208, 128), BF16),
        pltpu.SemaphoreType.DMA((10,)),
    ],
    [HBM, HBM, HBM],
    WIDE,
    HBM,
    "truncate",
)


def split_kernel(one_ref, other_ref, own_ref, gram):
    core = lax.axis_index("gz") % 2
    for c in range(4):
        gram[c * 512 : (c + 1) * 512, :] = one_ref[:, c * 128 : (c + 1) * 128]
    for out_ref, side in ((other_ref, 1 - core), (own_ref, core)):
        for b in range(8):
            for c in range(4):
                for e in range(2):
                    at = c * 32 + e * 16
                    rows = gram[pl.ds(c * 512 + b * 4 + side * 2 + e, 16, stride=32), :]
                    out_ref[b // 2, b % 2, at : at + 16, :] = rows.astype(BF16)


split = call(
    split_kernel,
    (shape((4, 2, 128, 128)), shape((4, 2, 128, 128))),
    [pltpu.VMEM((2048, 128), F32)],
    name="split",
)


def along_y_kernel(own_ref, got_ref, *out_refs):
    y = lax.axis_index("gz") // 4
    for distance, out_ref in enumerate(out_refs):
        at = lax.rem(y + distance, 4)
        out_ref[...] = (own_ref[at].astype(F32) + got_ref[at].astype(F32)).astype(BF16)


along_y = call(along_y_kernel, tuple(shape((2, 128, 128)) for _ in range(4)), name="along_y")


def along_z_kernel(*refs):
    other_ref, own_ref = refs[4:]
    place = lax.axis_index("gz") // 2 % 2
    for out_ref, at in ((other_ref, 1 - place), (own_ref, place)):
        total = refs[0][at].astype(F32)
        for ref in refs[1:4]:
            total = total + ref[at].astype(F32)
        out_ref[...] = total.astype(BF16)


along_z = call(along_z_kernel, (shape((128, 128)), shape((128, 128))), name="along_z")


def gram_rows(whole_ref, side, out_ref, gram):
    def cells(first, size):
        parts = [whole_ref[:, pl.ds(a * 32 + first, size), :] for a in range(6)]
        return jnp.concatenate([part.reshape(16 * size, 128) for part in parts], axis=1)

    values = nt_dot(cells(pl.multiple_of(side * 16, 16), 16), cells(0, 32))
    for c in range(4):
        gram[c * 256 : (c + 1) * 256, :] = values[:, c * 128 : (c + 1) * 128]
    for b in range(8):
        for c in range(4):
            rows = gram[pl.ds(c * 256 + b, 32, stride=8), :]
            out_ref[b, c * 32 : c * 32 + 32, :] = rows.astype(BF16)


def core_rows(kron_ref, high_ref, low_ref, side, out_ref):
    kron = kron_ref[pl.ds(pl.multiple_of(side * 384, 384), 384), :]
    parts = []
    for a in range(3):
        lanes = slice(a * 256, (a + 1) * 256)
        parts.append(nt_dot(kron, high_ref[:, lanes]) + nt_dot(kron, low_ref[:, lanes]))
    lane = lax.broadcasted_iota(jnp.int32, (112, 128), 1)
    for b in range(8):
        pieces = []
        for t in range(6):
            at = b * 48 + t * 8
            pieces += [part[at : at + 8] for part in parts]
        rest = jnp.concatenate(pieces[14:], axis=0)
        rest = [pltpu.roll(rest, 96 - 32 * g, 1) for g in range(3)]
        rest = jnp.concatenate(rest + [jnp.zeros((16, 128), F32)], axis=0)
        packed = jnp.where(lane < 96, jnp.concatenate(pieces[:14], axis=0), rest)
        out_ref[b] = packed.astype(out_ref.dtype)


def gram_kernel(whole_ref, after_ref, out_ref, gram):
    gram_rows(whole_ref, 1 - lax.axis_index("gz") % 2, out_ref, gram)


gram_part = call(
    gram_kernel,
    shape((8, 128, 128)),
    [pltpu.VMEM((1024, 128), F32)],
    [VMEM, ANY],
    name="gram_other",
)


def core_kernel(whole_ref, got_ref, kron_ref, *refs):
    out_ref, high_ref, low_ref, basis = refs[-4:]
    core = lax.axis_index("gz") % 2
    basis[:, core] = whole_ref[:, 192:208, :]
    basis[:, 1 - core] = got_ref[...]
    x = [whole_ref[:, a * 32 : (a + 1) * 32, :].reshape(512, 128) for a in range(6)]
    mixed = lax.dot_general(
        basis[...].reshape(512, 128),
        jnp.concatenate(x, axis=1),
        (((0,), (0,)), ((), ())),
        preferred_element_type=F32,
    )
    high_ref[...] = mixed.astype(BF16)
    low_ref[...] = (mixed - high_ref[...].astype(F32)).astype(BF16)
    core_rows(kron_ref, high_ref, low_ref, 1 - core, out_ref)


core_part = call(
    core_kernel,
    (shape((8, 112, 128)), shape((128, 768)), shape((128, 768))),
    [pltpu.VMEM((16, 2, 16, 128), BF16)],
    [VMEM, VMEM, VMEM, ANY, ANY],
    name="core_other",
)


def own_kernel(whole_ref, kron_ref, high_ref, low_ref, after_ref, gram_ref, core_ref, gram):
    core = lax.axis_index("gz") % 2
    gram_rows(whole_ref, core, gram_ref, gram)
    core_rows(kron_ref, high_ref, low_ref, core, core_ref)


own_part = call(
    own_kernel,
    (shape((8, 128, 128)), shape((8, 112, 128), F32)),
    [pltpu.VMEM((1024, 128), F32)],
    [VMEM] * 4 + [ANY],
    name="own",
)


def pair_kernel(gram_ref, gram_got_ref, core_ref, core_got_ref, out_ref):
    out_ref[:, 0:128, :] = (gram_ref[...].astype(F32) + gram_got_ref[...].astype(F32)).astype(BF16)
    out_ref[:, 128:240, :] = (core_ref[...] + core_got_ref[...].astype(F32)).astype(BF16)


pair = call(pair_kernel, shape((8, 240, 128)), name="pair")


def middle_kernel(in_ref, one_ref, one_got_ref, out_ref, sums, core, cut):
    total = in_ref[0].astype(F32)
    for source in range(1, 8):
        total = total + in_ref[source].astype(F32)
    sums[...] = total[0:128]
    cut[...] = jnp.zeros_like(cut)
    one = one_ref[...].astype(F32) + one_got_ref[...].astype(F32)
    for c in range(4):
        for e in range(2):
            at = c * 32 + e * 16
            cut[pl.ds(e * 4 + c, 16, stride=24), :] = one[at : at + 16]
            cut[pl.ds(8 + e * 4 + c, 16, stride=24), :] = sums[pl.ds(c * 32 + e, 16, stride=2), :]
    rest = [pltpu.roll(total[128 + g * 32 : 160 + g * 32], (32 + 32 * g) % 128, 1) for g in range(3)]
    lane = lax.broadcasted_iota(jnp.int32, (32, 128), 1)
    rest = jnp.where(lane < 32, rest[0], jnp.where(lane < 64, rest[1], rest[2]))
    core[0:128, :] = jnp.concatenate([total[128:240], rest[0:16]], axis=0).T
    tail = jnp.concatenate([rest[16:32], jnp.zeros((112, 128), F32)], axis=0)
    core[128:256, :] = tail.T
    lane = lax.broadcasted_iota(jnp.int32, (16, 128), 1) // 16
    last = jnp.zeros((16, 128), F32)
    for s in range(6):
        cut[pl.ds(16 + s, 16, stride=24), :] = core[pl.ds(s, 16, stride=6), :]
        part = core[pl.ds(128 + s, 16, stride=6), :]
        last = jnp.where(lane == s, pltpu.roll(part, 16 * s, 1) if s else part, last)
    cut[pl.ds(22, 16, stride=24), :] = last
    out_ref[...] = cut[...].reshape(16, 24, 128).astype(BF16)


middle = call(
    middle_kernel,
    shape((16, 24, 128)),
    [pltpu.VMEM((128, 128), F32), pltpu.VMEM((256, 128), F32), pltpu.VMEM((384, 128), F32)],
    name="middle",
)


def last_kernel(scale_one, scale_two, in_ref, one_ref, two_ref, core_ref, *scratch):
    turned, ordered, core, one_out, two_out, core_out, sems = scratch
    got = in_ref[...].astype(F32)
    lane = lax.broadcasted_iota(jnp.int32, (8, 128), 1)
    row = lax.broadcasted_iota(jnp.int32, (8, 128), 0)
    for v in range(4):
        blocks = [got[v * 4 + g, 16:24] for g in range(4)]
        for t in range(6):
            ranks = jnp.zeros((8, 128), F32)
            for g in range(4):
                shift = (24 * (g - t)) % 128
                moved = pltpu.roll(blocks[g], shift, 1) if shift else blocks[g]
                if t == 5:
                    rest = jnp.zeros((8, 128), F32)
                    for s in range(6):
                        turn = pltpu.roll(blocks[g], (24 * g + 8 - 16 * s) % 128, 1)
                        rest = jnp.where(row == s, turn[6:7], rest)
                    moved = jnp.where(lane < 24 * g + 8, moved, rest)
                ranks = jnp.where((lane >= 24 * g) & (lane < 24 * g + 24), moved, ranks)
            core[pl.ds(t * 4 + v, 8, stride=24), :] = ranks
    for s in range(6):
        for t in range(6):
            core_out[s, t] = core[(s * 6 + t) * 4 : (s * 6 + t) * 4 + 4, 0:96]
    copies = [pltpu.make_async_copy(core_out, core_ref, sems.at[0])]
    copies[0].start()
    total = got[0, 0:16]
    for source in range(1, 16):
        total = total + got[source, 0:16]
    turned[...] = jnp.concatenate([total[8:16], jnp.zeros((120, 128), F32)], axis=0).T
    for group in range(4):
        for jj in range(4):
            rows = turned[group * 32 + jj * 8 : group * 32 + jj * 8 + 8, :]
            ordered[pl.ds(group * 32 + jj, 8, stride=4), :] = rows
    two = ordered[...].T
    for e in range(2):
        for c in range(4):
            lanes = slice(c * 128, (c + 1) * 128)
            one_out[e : e + 1, lanes] = total[e * 4 + c : e * 4 + c + 1] * scale_one
            two_out[e : e + 1, lanes] = two[e * 4 + c : e * 4 + c + 1] * scale_two
    for held, out_ref in ((one_out, one_ref), (two_out, two_ref)):
        copies.append(pltpu.make_async_copy(held, out_ref, sems.at[len(copies)]))
        copies[-1].start()
    for copy in copies:
        copy.wait()


def last(received, scale_one, scale_two):
    def body(*refs):
        last_kernel(scale_one, scale_two, *refs)

    outs = ((2, 512), (2, 512), (6, 6, 4, 96))
    scratch = [pltpu.VMEM((rows, 128), F32) for rows in (128, 128, 192)]
    scratch += [pltpu.VMEM(dims, F32) for dims in outs] + [pltpu.SemaphoreType.DMA((3,))]
    outs = tuple(shape(dims, F32) for dims in outs)
    return call(body, outs, scratch, out_specs=(HBM,) * 3, name="last")(received)


def along_gz(y, z_lo, core):
    return [
        (i, (i // 4 + y) % 4 * 4 + (i // 2 % 2 ^ z_lo) * 2 + (i % 2 ^ core)) for i in range(16)
    ]


def send(block, y=0, z_lo=0, core=0):
    return lax.ppermute(block, "gz", along_gz(y, z_lo, core))


def shards(field, basis_one, basis_two, basis_three):
    sent = truncate(basis_one.T, basis_two, field)
    sent, field, basis_three = lax.optimization_barrier((sent, field, basis_three))
    whole = lax.all_to_all(sent, "gy", split_axis=0, concat_axis=0, tiled=True)

    flattened = field.reshape(-1, 512)
    one = jnp.dot(flattened.T, flattened, preferred_element_type=F32)
    other, own = split(one)
    blocks = along_y(own, send(other, core=1))
    blocks = [blocks[0]] + [send(blocks[d], y=d) for d in range(1, 4)]
    other, one_own = along_z(*blocks)
    one_got = send(other, z_lo=1)

    turned = jnp.transpose(basis_three.reshape(32, 8, 2, 6), (2, 1, 3, 0)).reshape(96, 32)
    repeated = jnp.tile(turned, (1, 8))[:, None, :]
    same = jnp.arange(8)[:, None] == jnp.arange(256)[None, :] // 32
    kron = jnp.where(same[None], repeated, jnp.zeros((), BF16)).reshape(768, 256)

    basis_got = send(whole[:, 192:208], core=1)
    gram_other = gram_part(whole, one_own)
    gram_got = send(gram_other, core=1)
    core_other, high, low = core_part(whole, basis_got, kron, gram_other, one_got)
    core_got = send(core_other, core=1)
    gram_own, core_own = own_part(whole, kron, high, low, core_other)
    summed = pair(gram_own, gram_got, core_own, core_got)
    groups = [[2 * b + core for b in range(8)] for core in range(2)]
    summed = lax.all_to_all(
        summed, "gz", split_axis=0, concat_axis=0, tiled=True, axis_index_groups=groups
    )
    cut = middle(summed, one_own, one_got)
    cut = lax.all_to_all(cut, "gy", split_axis=0, concat_axis=0, tiled=True)
    gram_one, gram_two, core = last(cut, 1.0 / 1048576, 1.0 / 196608)
    return (gram_one, gram_two, jnp.transpose(core, (2, 0, 1, 3)))


def solution(mesh):
    in_specs = (P(None, "gy", "gz", None), P(), P("gy", None), P("gz", None))
    out_specs = (P(("gy", "gz"), None), P(("gy", "gz"), None), P(None, "gy", "gz", None))
    return jax.shard_map(shards, mesh=mesh, in_specs=in_specs, out_specs=out_specs, check_vma=False)
```

```python
import functools

import jax
import jax.numpy as jnp
from jax import lax
from jax.experimental import pallas as pl
from jax.experimental.pallas import tpu as pltpu
from jax.sharding import PartitionSpec as P

F32 = jnp.float32
BF16 = jnp.bfloat16
WIDE = 60 * 1024 * 1024
LIMIT = 48 * 1024 * 1024
VMEM = pl.BlockSpec(memory_space=pltpu.VMEM)
HBM = pl.BlockSpec(memory_space=pltpu.HBM)
ANY = pl.BlockSpec(memory_space=pl.ANY)


def nt_dot(a, b):
    return lax.dot_general(a, b, (((1,), (1,)), ((), ())), preferred_element_type=F32)


def call(kernel, outs, scratch=(), specs=None, limit=LIMIT, out_specs=None, name=None):
    keywords = {} if out_specs is None else {"out_specs": out_specs}
    return lambda *args: pl.pallas_call(
        kernel,
        out_shape=outs,
        in_specs=[VMEM] * len(args) if specs is None else specs,
        scratch_shapes=list(scratch),
        compiler_params=pltpu.CompilerParams(vmem_limit_bytes=limit),
        name=name,
        **keywords,
    )(*args)


def shape(dims, dtype=BF16):
    return jax.ShapeDtypeStruct(dims, dtype)


def truncate_kernel(b1t_ref, b2_ref, field_ref, out_ref, *scratch):
    b1t, b2, b2_wide, cells, *work, sent, sems = scratch
    core = lax.axis_index("gz") % 2
    small = [
        pltpu.make_async_copy(b1t_ref, b1t, sems.at[0]),
        pltpu.make_async_copy(b2_ref, b2, sems.at[1]),
    ]
    copies = [pltpu.make_async_copy(field_ref.at[v], cells.at[v], sems.at[2 + v]) for v in range(4)]
    for copy in small + copies:
        copy.start()
    for copy in small:
        copy.wait()
    b2_wide[...] = jnp.zeros_like(b2_wide)
    b2_wide[:, 0:96] = b2[...].astype(F32)
    share = [b2_wide[pl.ds(core * 2 + e, 8, stride=4), :] for e in range(2)]
    share = jnp.concatenate(share, axis=0).astype(BF16)
    for peer in range(16):
        sent[peer, 192:208, :] = share
    lane = lax.broadcasted_iota(jnp.int32, (8, 128), 1) // 32

    def product(v):
        rows = work[v % 2]
        trunc = nt_dot(b1t[...], cells[v].reshape(1024, 512))
        for b in range(8):
            rows[pl.ds(b, 96, stride=8), :] = trunc[:, b * 128 : (b + 1) * 128]

    def arrange(v):
        rows, tiles = work[v % 2], work[2 + v % 2]
        for block in range(24):
            first = block * 32
            part = [rows[first + rr * 8 : first + rr * 8 + 8, :] for rr in range(4)]
            for jj in range(4):
                moved = [
                    part[rr] if rr == jj else pltpu.roll(part[rr], (32 * (rr - jj)) % 128, 1)
                    for rr in range(4)
                ]
                low = jnp.where(lane == 0, moved[0], moved[1])
                high = jnp.where(lane == 2, moved[2], moved[3])
                tiles[first + jj * 8 : first + jj * 8 + 8, :] = jnp.where(lane < 2, low, high)
        sent[v * 4 : v * 4 + 4, 0:192, :] = tiles[...].astype(BF16).reshape(4, 192, 128)

    outs = []
    for v in range(5):
        if v < 4:
            copies[v].wait()
            product(v)
        if v > 0:
            arrange(v - 1)
            block = slice(v * 4 - 4, v * 4)
            outs.append(pltpu.make_async_copy(sent.at[block], out_ref.at[block], sems.at[5 + v]))
            outs[-1].start()
    for copy in outs:
        copy.wait()


truncate = call(
    truncate_kernel,
    shape((16, 208, 128)),
    [
        pltpu.VMEM((96, 512), BF16),
        pltpu.VMEM((32, 96), BF16),
        pltpu.VMEM((32, 128), F32),
        pltpu.VMEM((4, 32, 32, 512), BF16),
        *[pltpu.VMEM((768, 128), F32)] * 4,
        pltpu.VMEM((16, 208, 128), BF16),
        pltpu.SemaphoreType.DMA((10,)),
    ],
    [HBM, HBM, HBM],
    WIDE,
    HBM,
    "truncate",
)


def split_kernel(one_ref, other_ref, own_ref, gram):
    core = lax.axis_index("gz") % 2
    for c in range(4):
        gram[c * 512 : (c + 1) * 512, :] = one_ref[:, c * 128 : (c + 1) * 128]
    for out_ref, side in ((other_ref, 1 - core), (own_ref, core)):
        for b in range(8):
            for c in range(4):
                for e in range(2):
                    at = c * 32 + e * 16
                    rows = gram[pl.ds(c * 512 + b * 4 + side * 2 + e, 16, stride=32), :]
                    out_ref[b // 2, b % 2, at : at + 16, :] = rows.astype(BF16)


split = call(
    split_kernel,
    (shape((4, 2, 128, 128)), shape((4, 2, 128, 128))),
    [pltpu.VMEM((2048, 128), F32)],
    name="split",
)


def along_y_kernel(own_ref, got_ref, *out_refs):
    y = lax.axis_index("gz") // 4
    for distance, out_ref in enumerate(out_refs):
        at = lax.rem(y + distance, 4)
        out_ref[...] = (own_ref[at].astype(F32) + got_ref[at].astype(F32)).astype(BF16)


along_y = call(along_y_kernel, tuple(shape((2, 128, 128)) for _ in range(4)), name="along_y")


def along_z_kernel(*refs):
    other_ref, own_ref = refs[4:]
    place = lax.axis_index("gz") // 2 % 2
    for out_ref, at in ((other_ref, 1 - place), (own_ref, place)):
        total = refs[0][at].astype(F32)
        for ref in refs[1:4]:
            total = total + ref[at].astype(F32)
        out_ref[...] = total.astype(BF16)


along_z = call(along_z_kernel, (shape((128, 128)), shape((128, 128))), name="along_z")


def gram_rows(whole_ref, side, out_ref, gram):
    def cells(first, size):
        parts = [whole_ref[:, pl.ds(a * 32 + first, size), :] for a in range(6)]
        return jnp.concatenate([part.reshape(16 * size, 128) for part in parts], axis=1)

    mine, whole = cells(pl.multiple_of(side * 16, 16), 16), cells(0, 32)
    for half in range(2):
        values = nt_dot(mine, whole[half * 256 : half * 256 + 256])
        for c in range(half * 2, half * 2 + 2):
            at = c % 2 * 128
            gram[c * 256 : (c + 1) * 256, :] = values[:, at : at + 128]
            for b in range(8):
                rows = gram[pl.ds(c * 256 + b, 32, stride=8), :]
                out_ref[b, c * 32 : c * 32 + 32, :] = rows.astype(BF16)


def core_rows(kron_ref, high_ref, low_ref, side, out_ref):
    kron = kron_ref[pl.ds(pl.multiple_of(side * 384, 384), 384), :]
    parts = []
    for a in range(3):
        lanes = slice(a * 256, (a + 1) * 256)
        parts.append(nt_dot(kron, high_ref[:, lanes]) + nt_dot(kron, low_ref[:, lanes]))
    lane = lax.broadcasted_iota(jnp.int32, (112, 128), 1)
    for b in range(8):
        pieces = []
        for t in range(6):
            at = b * 48 + t * 8
            pieces += [part[at : at + 8] for part in parts]
        rest = jnp.concatenate(pieces[14:], axis=0)
        rest = [pltpu.roll(rest, 96 - 32 * g, 1) for g in range(3)]
        rest = jnp.concatenate(rest + [jnp.zeros((16, 128), F32)], axis=0)
        packed = jnp.where(lane < 96, jnp.concatenate(pieces[:14], axis=0), rest)
        out_ref[b] = packed.astype(out_ref.dtype)


def gram_kernel(whole_ref, after_ref, out_ref, gram):
    gram_rows(whole_ref, 1 - lax.axis_index("gz") % 2, out_ref, gram)


gram_part = call(
    gram_kernel,
    shape((8, 128, 128)),
    [pltpu.VMEM((1024, 128), F32)],
    [VMEM, ANY],
    name="gram_other",
)


def core_kernel(whole_ref, got_ref, kron_ref, *refs):
    out_ref, high_ref, low_ref, basis = refs[-4:]
    core = lax.axis_index("gz") % 2
    basis[:, core] = whole_ref[:, 192:208, :]
    basis[:, 1 - core] = got_ref[...]
    x = [whole_ref[:, a * 32 : (a + 1) * 32, :].reshape(512, 128) for a in range(6)]
    mixed = lax.dot_general(
        basis[...].reshape(512, 128),
        jnp.concatenate(x, axis=1),
        (((0,), (0,)), ((), ())),
        preferred_element_type=F32,
    )
    high_ref[...] = mixed.astype(BF16)
    low_ref[...] = (mixed - high_ref[...].astype(F32)).astype(BF16)
    core_rows(kron_ref, high_ref, low_ref, 1 - core, out_ref)


core_part = call(
    core_kernel,
    (shape((8, 112, 128)), shape((128, 768)), shape((128, 768))),
    [pltpu.VMEM((16, 2, 16, 128), BF16)],
    [VMEM, VMEM, VMEM, ANY, ANY],
    name="core_other",
)


def own_kernel(whole_ref, kron_ref, high_ref, low_ref, after_ref, gram_ref, core_ref, gram):
    core = lax.axis_index("gz") % 2
    gram_rows(whole_ref, core, gram_ref, gram)
    core_rows(kron_ref, high_ref, low_ref, core, core_ref)


own_part = call(
    own_kernel,
    (shape((8, 128, 128)), shape((8, 112, 128), F32)),
    [pltpu.VMEM((1024, 128), F32)],
    [VMEM] * 4 + [ANY],
    name="own",
)


def pair_kernel(gram_ref, gram_got_ref, core_ref, core_got_ref, out_ref):
    out_ref[:, 0:128, :] = (gram_ref[...].astype(F32) + gram_got_ref[...].astype(F32)).astype(BF16)
    out_ref[:, 128:240, :] = (core_ref[...] + core_got_ref[...].astype(F32)).astype(BF16)


pair = call(pair_kernel, shape((8, 240, 128)), name="pair")


def middle_kernel(in_ref, one_ref, one_got_ref, out_ref, sums, core, cut):
    total = in_ref[0].astype(F32)
    for source in range(1, 8):
        total = total + in_ref[source].astype(F32)
    sums[...] = total[0:128]
    cut[...] = jnp.zeros_like(cut)
    one = one_ref[...].astype(F32) + one_got_ref[...].astype(F32)
    for c in range(4):
        for e in range(2):
            at = c * 32 + e * 16
            cut[pl.ds(e * 4 + c, 16, stride=24), :] = one[at : at + 16]
            cut[pl.ds(8 + e * 4 + c, 16, stride=24), :] = sums[pl.ds(c * 32 + e, 16, stride=2), :]
    rest = [pltpu.roll(total[128 + g * 32 : 160 + g * 32], (32 + 32 * g) % 128, 1) for g in range(3)]
    lane = lax.broadcasted_iota(jnp.int32, (32, 128), 1)
    rest = jnp.where(lane < 32, rest[0], jnp.where(lane < 64, rest[1], rest[2]))
    core[0:128, :] = jnp.concatenate([total[128:240], rest[0:16]], axis=0).T
    tail = jnp.concatenate([rest[16:32], jnp.zeros((112, 128), F32)], axis=0)
    core[128:256, :] = tail.T
    lane = lax.broadcasted_iota(jnp.int32, (16, 128), 1) // 16
    last = jnp.zeros((16, 128), F32)
    for s in range(6):
        cut[pl.ds(16 + s, 16, stride=24), :] = core[pl.ds(s, 16, stride=6), :]
        part = core[pl.ds(128 + s, 16, stride=6), :]
        last = jnp.where(lane == s, pltpu.roll(part, 16 * s, 1) if s else part, last)
    cut[pl.ds(22, 16, stride=24), :] = last
    out_ref[...] = cut[...].reshape(16, 24, 128).astype(BF16)


middle = call(
    middle_kernel,
    shape((16, 24, 128)),
    [pltpu.VMEM((128, 128), F32), pltpu.VMEM((256, 128), F32), pltpu.VMEM((384, 128), F32)],
    name="middle",
)


def last_kernel(scale_one, scale_two, in_ref, one_ref, two_ref, core_ref, *scratch):
    turned, ordered, core, one_out, two_out, core_out, sems = scratch
    got = in_ref[...].astype(F32)
    lane = lax.broadcasted_iota(jnp.int32, (8, 128), 1)
    row = lax.broadcasted_iota(jnp.int32, (8, 128), 0)
    for v in range(4):
        blocks = [got[v * 4 + g, 16:24] for g in range(4)]
        for t in range(6):
            ranks = jnp.zeros((8, 128), F32)
            for g in range(4):
                shift = (24 * (g - t)) % 128
                moved = pltpu.roll(blocks[g], shift, 1) if shift else blocks[g]
                if t == 5:
                    rest = jnp.zeros((8, 128), F32)
                    for s in range(6):
                        turn = pltpu.roll(blocks[g], (24 * g + 8 - 16 * s) % 128, 1)
                        rest = jnp.where(row == s, turn[6:7], rest)
                    moved = jnp.where(lane < 24 * g + 8, moved, rest)
                ranks = jnp.where((lane >= 24 * g) & (lane < 24 * g + 24), moved, ranks)
            core[pl.ds(t * 4 + v, 8, stride=24), :] = ranks
    for s in range(6):
        for t in range(6):
            core_out[s, t] = core[(s * 6 + t) * 4 : (s * 6 + t) * 4 + 4, 0:96]
    copies = [pltpu.make_async_copy(core_out, core_ref, sems.at[0])]
    copies[0].start()
    total = got[0, 0:16]
    for source in range(1, 16):
        total = total + got[source, 0:16]
    turned[...] = jnp.concatenate([total[8:16], jnp.zeros((120, 128), F32)], axis=0).T
    for group in range(4):
        for jj in range(4):
            rows = turned[group * 32 + jj * 8 : group * 32 + jj * 8 + 8, :]
            ordered[pl.ds(group * 32 + jj, 8, stride=4), :] = rows
    two = ordered[...].T
    for e in range(2):
        for c in range(4):
            lanes = slice(c * 128, (c + 1) * 128)
            one_out[e : e + 1, lanes] = total[e * 4 + c : e * 4 + c + 1] * scale_one
            two_out[e : e + 1, lanes] = two[e * 4 + c : e * 4 + c + 1] * scale_two
    for held, out_ref in ((one_out, one_ref), (two_out, two_ref)):
        copies.append(pltpu.make_async_copy(held, out_ref, sems.at[len(copies)]))
        copies[-1].start()
    for copy in copies:
        copy.wait()


def last(received, scale_one, scale_two):
    def body(*refs):
        last_kernel(scale_one, scale_two, *refs)

    outs = ((2, 512), (2, 512), (6, 6, 4, 96))
    scratch = [pltpu.VMEM((rows, 128), F32) for rows in (128, 128, 192)]
    scratch += [pltpu.VMEM(dims, F32) for dims in outs] + [pltpu.SemaphoreType.DMA((3,))]
    outs = tuple(shape(dims, F32) for dims in outs)
    return call(body, outs, scratch, out_specs=(HBM,) * 3, name="last")(received)


def along_gz(y, z_lo, core):
    return [
        (i, (i // 4 + y) % 4 * 4 + (i // 2 % 2 ^ z_lo) * 2 + (i % 2 ^ core)) for i in range(16)
    ]


def send(block, y=0, z_lo=0, core=0):
    return lax.ppermute(block, "gz", along_gz(y, z_lo, core))


def shards(field, basis_one, basis_two, basis_three):
    sent = truncate(basis_one.T, basis_two, field)
    sent, field, basis_three = lax.optimization_barrier((sent, field, basis_three))
    whole = lax.all_to_all(sent, "gy", split_axis=0, concat_axis=0, tiled=True)

    flattened = field.reshape(-1, 512)
    one = jnp.dot(flattened.T, flattened, preferred_element_type=F32)
    other, own = split(one)
    blocks = along_y(own, send(other, core=1))
    blocks = [blocks[0]] + [send(blocks[d], y=d) for d in range(1, 4)]
    other, one_own = along_z(*blocks)
    one_got = send(other, z_lo=1)

    turned = jnp.transpose(basis_three.reshape(32, 8, 2, 6), (2, 1, 3, 0)).reshape(96, 32)
    repeated = jnp.tile(turned, (1, 8))[:, None, :]
    same = jnp.arange(8)[:, None] == jnp.arange(256)[None, :] // 32
    kron = jnp.where(same[None], repeated, jnp.zeros((), BF16)).reshape(768, 256)

    basis_got = send(whole[:, 192:208], core=1)
    gram_other = gram_part(whole, one_own)
    gram_got = send(gram_other, core=1)
    core_other, high, low = core_part(whole, basis_got, kron, gram_other, one_got)
    core_got = send(core_other, core=1)
    gram_own, core_own = own_part(whole, kron, high, low, core_other)
    summed = pair(gram_own, gram_got, core_own, core_got)
    groups = [[2 * b + core for b in range(8)] for core in range(2)]
    summed = lax.all_to_all(
        summed, "gz", split_axis=0, concat_axis=0, tiled=True, axis_index_groups=groups
    )
    cut = middle(summed, one_own, one_got)
    cut = lax.all_to_all(cut, "gy", split_axis=0, concat_axis=0, tiled=True)
    gram_one, gram_two, core = last(cut, 1.0 / 1048576, 1.0 / 196608)
    return (gram_one, gram_two, jnp.transpose(core, (2, 0, 1, 3)))


def solution(mesh):
    in_specs = (P(None, "gy", "gz", None), P(), P("gy", None), P("gz", None))
    out_specs = (P(("gy", "gz"), None), P(("gy", "gz"), None), P(None, "gy", "gz", None))
    return jax.shard_map(shards, mesh=mesh, in_specs=in_specs, out_specs=out_specs, check_vma=False)
```
